32 devices in a mesh: section: 2 (over core), dp: 16 (over z, y, x).
Axes of the slice: x: 2, y: 2, z: 4, core: 2. Of those that a mesh axis runs over, the one named last changes fastest.
Arguments:
- boundary: bfloat16 [2, 2, 8192, 256], P('section', None, 'dp'), may hold values from -6 to 6
- stencil_weight: float32 [2, 27, 256, 256], P('section', None, 'dp'), may hold values from -0.078125 to 0.078125
- mixing_weight: float32 [2, 256, 256], P('section', 'dp'), may hold values from -0.375 to 0.375
- project_in: float32 [2, 256, 768], P('section', 'dp'), may hold values from -0.375 to 0.375
- project_out: float32 [2, 256, 256], P('section', 'dp'), may hold values from -1 to 1
- expand_weight: float32 [2, 256, 1024], P('section', 'dp'), may hold values from -0.375 to 0.375
- reduce_weight: float32 [2, 1024, 256], P('section', 'dp'), may hold values from -0.1875 to 0.1875
- norm_gains: float32 [2, 3, 256], P('section', None, 'dp'), may hold values from 0.5 to 1.5
- bias_rows: float32 [2, 9, 256], P('section', None, 'dp'), may hold values from -2 to 2
- expand_bias: float32 [2, 1024], P('section', 'dp'), may hold values from -2 to 2
- patch_index: int32 [2, 2, 8192, 1], P('section', None, 'dp'), may hold values from 0 to 15; in each aligned block of 512 rows (0 to 511, 512 to 1023, ..., all dimensions but the last counted through in order) at most 48 rows name the same one
- neighbors: int32 [2, 8192, 27], P(None, 'dp'), may hold values from -1 to 8191, as said below
Outputs:
- boundary_out: float32 [2, 2, 8192, 256], P('section', None, 'dp')
- stencil_grad: float32 [2, 27, 256, 256], P('section', None, 'dp')
- mixing_grad: float32 [2, 256, 256], P('section', 'dp')
- project_in_grad: float32 [2, 256, 768], P('section', 'dp')
- project_out_grad: float32 [2, 256, 256], P('section', 'dp')
- expand_grad: float32 [2, 256, 1024], P('section', 'dp')
- reduce_grad: float32 [2, 1024, 256], P('section', 'dp')
- gains_grad: float32 [2, 3, 256], P('section', None, 'dp')
- biases_grad: float32 [2, 9, 256], P('section', None, 'dp')
- expand_bias_grad: float32 [2, 1024], P('section', 'dp')
The draws below stay inside these ranges and needn't reach their ends.
Inputs may be any that keep to these rules, and one draw needn't show every extreme that they name: `patch_index`: of the points of one device in one block and micro-batch, at most 48 share a patch, and some patch gets exactly 48. `neighbors`: A neighbour lies within 64 positions of its point in storage order; slot 13 is the point itself; -1 marks an absent neighbour.
All inputs are finite; a program needn't handle non-finite values.
Results may differ from the reference program's by a relative error of at most 0.014.
Values may be sent and summed in bfloat16 or wider, within the bound.
No kernel may reach another device: no remote copies, remote signals or barrier semaphores. Data moves between devices by JAX's collectives and lax.ppermute only.
A program may use at most 256 MiB of HBM per device.

```python
import math
import jax
import jax.numpy as jnp
import numpy as np
from jax import lax

D = 256
HEADS = 16
FF = 1024
KERNEL = 27
ROWS = 512
MB = 2
HALO = 64
HEAD_DIM = 16
CAP = 48
SLOTS = 768
POINTS = 8192
N_DP = 16


def draw_neighbors(key, part):
    key = jax.random.fold_in(key, 11)
    first, second = jax.random.split(key)
    offsets = jax.random.randint(first, (MB, POINTS, KERNEL), -HALO, HALO + 1)
    kept = jax.random.randint(second, (MB, POINTS, KERNEL), 0, 5) < 3
    column = jnp.arange(KERNEL)
    offsets = jnp.where(column == 0, -HALO, jnp.where(column == KERNEL - 1, HALO, jnp.where(column == KERNEL // 2, 0, offsets)))
    kept = kept | (column == KERNEL // 2)
    target = jnp.arange(POINTS)[None, :, None] + offsets
    inside = (target >= 0) & (target < POINTS)
    return jnp.where(kept & inside, target, -1).astype(jnp.int32)


def level_of(key, dims, shards, low, largest):
    factor_of, own = 1.0, jax.random.fold_in(key, 6)
    for position, blocks in shards:
        draws = jnp.exp(jax.random.uniform(jax.random.fold_in(own, position), (blocks,), jnp.float32, low / len(shards), largest / len(shards)))
        factor_of = factor_of * jnp.repeat(draws, dims[position] // blocks).reshape([-1 if axis == position else 1 for axis in range(len(dims))])
    return factor_of


def routed_block(stream_key, own, number, rows, count, top, most, slope):
    order = jax.random.permutation(stream_key, count)
    heavy_load, common = shares(count, rows * top, most, slope, True), shares(count, rows * top, most, slope, False)
    places = jnp.arange(count)

    def named(sizes, turn):
        used = int((sizes > 0).sum())
        fixed = max(1, used // 4)
        shifted = fixed + (places - fixed + turn * (used - fixed)) % max(1, count - fixed)
        return jnp.zeros((count,), jnp.int32).at[order[jnp.where(places < fixed, places, shifted)]].set(jnp.asarray(sizes, jnp.int32))

    sizes = jnp.where(number % 4 == 0, named(heavy_load, number // 4), named(common, number - number // 4 - 1))
    mixed = jax.random.permutation(jax.random.fold_in(own, 3), count)
    giver, taker = mixed[0:count // 2 * 2:2], mixed[1:count // 2 * 2:2]
    margin = jnp.minimum(sizes[giver] - 1, most - sizes[taker]) // 2
    margin = jnp.where((giver == order[0]) | (taker == order[0]) | (sizes[taker] == 0), 0, jnp.maximum(margin, 0))
    shifted = jax.random.randint(jax.random.fold_in(own, 4), (count // 2,), 0, 1 << 20) % (margin + 1)
    sizes = sizes.at[giver].add(-shifted).at[taker].add(shifted)
    items = jnp.searchsorted(jnp.cumsum(sizes), jnp.arange(rows * top), side="right").astype(jnp.int32)
    table = items.reshape(top, rows).T
    table = table[jax.random.permutation(jax.random.fold_in(own, 1), rows)]
    turn = jax.random.randint(jax.random.fold_in(own, 2), (rows, 1), 0, top)
    return jnp.take_along_axis(table, (jnp.arange(top)[None, :] + turn) % top, axis=1)


def shares(number_of, total, reach, slope, full):
    weights = [(1 << 20) // math.isqrt(grade ** slope) + 1 for grade in range(1, number_of + 1)]
    largest = reach if full else min(reach, max(-(-total // number_of), total * weights[0] // sum(weights)))
    least = 1 if total - largest >= number_of - 1 else 0
    holding, surplus = [largest] + [least] * (number_of - 1), total - largest - least * (number_of - 1)
    while surplus > 0:
        free = [i for i in range(1, number_of) if holding[i] < largest] or [i for i in range(1, number_of) if holding[i] < reach]
        whole, budget = sum([weights[i] for i in free]), surplus
        for i in free:
            more = min(reach - holding[i], max(1, budget * weights[i] // whole), surplus)
            holding[i] = holding[i] + more
            surplus = surplus - more
    return np.array(holding)


def gaussian(rng, dims, deviation, limit, shards=(), kind=jnp.bfloat16):
    result = deviation * jax.random.normal(rng, dims, jnp.float32)
    if shards:
        result = result * level_of(rng, dims, shards, -0.22, 0.18)
    return jnp.clip(result, -limit, limit).astype(kind)


def setup_inputs(seed: int = 0) -> dict:
    splits = jax.random.split(jax.random.key(seed), 13)
    boundary = gaussian(splits[0], (2, MB, POINTS, D), 1.0, 6.0, ((0, 2), (2, 16)))
    stencil_weight = gaussian(splits[1], (2, KERNEL, D, D), (KERNEL * D) ** -0.5, 0.078125, ((0, 2), (2, 16)), jnp.float32)
    mixing_weight = gaussian(splits[2], (2, D, D), D ** -0.5, 0.375, ((0, 2), (1, 16)), jnp.float32)
    project_in = gaussian(splits[3], (2, D, 3 * D), D ** -0.5, 0.375, ((0, 2), (1, 16)), jnp.float32)
    project_out = gaussian(splits[4], (2, D, D), (D // 8) ** -0.5, 1.0, ((0, 2), (1, 16)), jnp.float32)
    expand_weight = gaussian(splits[5], (2, D, FF), D ** -0.5, 0.375, ((0, 2), (1, 16)), jnp.float32)
    reduce_weight = gaussian(splits[6], (2, FF, D), FF ** -0.5, 0.1875, ((0, 2), (1, 16)), jnp.float32)
    norm_gains = jnp.clip(1.0 + 0.1 * jax.random.normal(splits[7], (2, 3, D), jnp.float32), 0.5, 1.5)
    bias_rows = gaussian(splits[8], (2, 9, D), 0.3, 2.0, ((0, 2), (2, 16)), jnp.float32)
    expand_bias = gaussian(splits[9], (2, FF), 0.3, 2.0, ((0, 2), (1, 16)), jnp.float32)
    patch_index_keys = jax.random.split(jax.random.fold_in(splits[10], 1), 2 * MB * POINTS // ROWS)
    patch_index_turns = jax.random.permutation(jax.random.fold_in(splits[10], 3), 2 * MB * POINTS // ROWS)
    patch_index = jax.vmap(lambda own, number: routed_block(jax.random.fold_in(splits[10], 2), own, number, ROWS, N_DP, 1, CAP, 1))(patch_index_keys, patch_index_turns).reshape((2, MB, POINTS, 1))
    neighbors = draw_neighbors(jax.random.fold_in(splits[12], 71), 0)
    return {"boundary": boundary, "stencil_weight": stencil_weight, "mixing_weight": mixing_weight, "project_in": project_in, "project_out": project_out, "expand_weight": expand_weight, "reduce_weight": reduce_weight, "norm_gains": norm_gains, "bias_rows": bias_rows, "expand_bias": expand_bias, "patch_index": patch_index, "neighbors": neighbors}


EPS = 1e-05
NEGATIVE = -1e+30

@jax.custom_vjp
def low(v):
    return lax.optimization_barrier(v.astype(jnp.bfloat16)).astype(jnp.float32)

@jax.custom_vjp
def low_back(v):
    return v

def low_keep(v):
    return (low(v), None)

def low_pass(kept, grad):
    return (grad,)

def back_keep(v):
    return (v, None)

def back_low(kept, grad):
    return (low(grad),)
low.defvjp(low_keep, low_pass)
low_back.defvjp(back_keep, back_low)

def norm_rows(inputs, scales, offsets):
    average = lax.optimization_barrier(jnp.mean(inputs, axis=-1, keepdims=True))
    centred = inputs - average
    spread = lax.optimization_barrier(jnp.mean(centred * centred, axis=-1, keepdims=True))
    return centred * lax.rsqrt(spread + EPS) * scales + offsets

def product(left, right):
    return jnp.dot(left, right, precision=lax.Precision.HIGHEST, preferred_element_type=jnp.float32)

def matmul(left, right):
    return low_back(product(low(left), right))

def slot_table(target, capacity, groups):
    one_hot = (target[:, None] == jnp.arange(groups, dtype=jnp.int32)[None, :]).astype(jnp.int32)
    before = jnp.cumsum(one_hot, axis=0) - one_hot
    order = lax.optimization_barrier(jnp.sum(before * one_hot, axis=1))
    place = target * capacity + order
    source = jnp.full((groups * capacity,), -1, jnp.int32).at[place].set(jnp.arange(target.shape[0], dtype=jnp.int32))
    return (place, source)

def routing(targets):
    place, source = jax.vmap(lambda row: slot_table(row, CAP, N_DP))(targets.reshape(N_DP, ROWS))
    base = (jnp.arange(N_DP, dtype=jnp.int32) * ROWS)[:, None]
    present = source >= 0
    where_from = jnp.where(present, source + base, 0).astype(jnp.int32)
    gather_index = jnp.transpose(where_from.reshape(N_DP, N_DP, CAP), (1, 0, 2)).reshape(N_DP, SLOTS)
    flags = jnp.transpose(present.reshape(N_DP, N_DP, CAP), (1, 0, 2)).reshape(N_DP, SLOTS)
    owner = place // CAP
    within = place % CAP
    home = jnp.arange(N_DP, dtype=jnp.int32)[:, None]
    back_index = (owner * SLOTS + home * CAP + within).reshape(POINTS).astype(jnp.int32)
    return (gather_index, flags, back_index)

def patch_attention(patch, flags, weight, query_bias, value_bias):
    mixed = matmul(patch, weight)
    query = low(mixed[:, :D] + query_bias).reshape(SLOTS, HEADS, HEAD_DIM)
    keys = low(mixed[:, D:2 * D]).reshape(SLOTS, HEADS, HEAD_DIM)
    values = low(mixed[:, 2 * D:] + value_bias).reshape(SLOTS, HEADS, HEAD_DIM)
    scores = low_back(jnp.einsum('qhd,khd->hqk', query, keys, precision=lax.Precision.HIGHEST))
    scores = jnp.where(flags[None, None, :], scores * HEAD_DIM ** (-0.5), NEGATIVE)
    probs = jax.nn.softmax(scores, axis=-1)
    out = jnp.einsum('hqk,khd->qhd', low(probs), values, precision=lax.Precision.HIGHEST)
    return low_back(low(out.reshape(SLOTS, D)))

def block(inputs, params, targets, linked):
    stencil, mixing, proj_in, proj_out, expand, reduce_w, gains, biases, expand_b = params
    rounded = low_back(low(inputs))
    valid = linked >= 0
    picked = jnp.where(valid[:, :, None], rounded[jnp.maximum(linked, 0)], 0.0)
    conv_out = low_back(product(picked.reshape(POINTS, KERNEL * D), stencil.reshape(KERNEL * D, D)))
    first = conv_out + biases[0]
    second = matmul(first, mixing) + biases[1]
    after_cpe = inputs + norm_rows(second, gains[0], biases[2])
    normed = low_back(low(norm_rows(after_cpe, gains[1], biases[3])))
    gather_index, flags, back_index = routing(targets)
    patches = jnp.where(flags[:, :, None], normed[gather_index], 0.0)
    attend = jax.checkpoint(lambda pieces: patch_attention(pieces[0], pieces[1], proj_in, biases[4], biases[5]))
    attended = lax.map(attend, (patches, flags))
    mixed_rows = attended.reshape(N_DP * SLOTS, D)[back_index]
    after_attn = after_cpe + matmul(mixed_rows, proj_out) + biases[6]
    hidden = low(norm_rows(after_attn, gains[2], biases[7]))
    gated = low(jax.nn.gelu(matmul(hidden, expand) + expand_b, approximate=False))
    return after_attn + matmul(gated, reduce_w) + biases[8]

def reference(boundary, stencil_weight, mixing_weight, project_in, project_out, expand_weight, reduce_weight, norm_gains, bias_rows, expand_bias, patch_index, neighbors):
    masters = (stencil_weight, mixing_weight, project_in, project_out, expand_weight, reduce_weight, norm_gains, bias_rows, expand_bias)
    inputs = boundary[0].astype(jnp.float32)
    cotangent = boundary[1].astype(jnp.float32)

    def forward(features, weights):
        params = tuple((low(item) for item in weights))
        results = []
        for micro in range(MB):
            first = block(features[micro], tuple((item[0] for item in params)), patch_index[0, micro, :, 0], neighbors[micro])
            first = low_back(low(first))
            results.append(block(first, tuple((item[1] for item in params)), patch_index[1, micro, :, 0], neighbors[micro]))
        return jnp.stack(results)
    output, pullback = jax.vjp(forward, inputs, masters)
    grad_in, grads = pullback(cotangent)
    return (jnp.stack([grad_in, output]), grads[0], grads[1], grads[2], grads[3], grads[4], grads[5], grads[6], grads[7], grads[8])
```

```python
import functools
import math

import jax
import jax.numpy as jnp
from jax import lax
from jax.experimental import pallas as pl
from jax.experimental.pallas import tpu as pltpu
from jax.sharding import PartitionSpec as P

HEADS = 16
HALO = 64
EPS = 1e-05
NEGATIVE = -1e30
LOWEST = -1e29
LOG2E = 1.4426950408889634
BLOCK = 128
WINDOW = BLOCK + 2 * HALO
LANES = 128
WIDTH = 256
STEP = 256
ABSENT = -(1 << 20)
NEAR = 4
POINTS = ("far", "near")
F32 = jnp.float32
BF16 = jnp.bfloat16


def dot(left, right):
    return jnp.dot(left, right, preferred_element_type=F32)


def dot_tn(left, right):
    return lax.dot_general(left, right, (((0,), (0,)), ((), ())), preferred_element_type=F32)


def dot_nt(left, right):
    return lax.dot_general(left, right, (((1,), (1,)), ((), ())), preferred_element_type=F32)


def dot_tt(left, right):
    return lax.dot_general(left, right, (((0,), (1,)), ((), ())), preferred_element_type=F32)


def iota(shape, dim):
    return lax.broadcasted_iota(jnp.int32, shape, dim)


def norm_parts(rows):
    centred = rows - jnp.mean(rows, axis=-1, keepdims=True)
    spread = jnp.mean(centred * centred, axis=-1, keepdims=True)
    scale = lax.rsqrt(spread + EPS)
    return centred * scale, scale


def norm(rows, gain, shift):
    return norm_parts(rows)[0] * gain + shift


def norm_back(unit, scale, gain, grad):
    inner = grad * gain
    first = jnp.mean(inner, axis=-1, keepdims=True)
    second = jnp.mean(inner * unit, axis=-1, keepdims=True)
    rows = scale * (inner - first - unit * second)
    return rows, column_sum(grad * unit), column_sum(grad)


def column_sum(rows):
    return jnp.sum(rows, axis=0, keepdims=True)


def gelu_parts(inputs):
    cdf = 0.5 + 0.5 * lax.erf(inputs * (0.5**0.5))
    density = jnp.exp(inputs * inputs * -0.5) * (1.0 / math.sqrt(2.0 * math.pi))
    return inputs * cdf, cdf + inputs * density


def gelu(inputs):
    return inputs * (0.5 + 0.5 * lax.erf(inputs * (0.5**0.5)))


GAIN = 0
BIAS = 3


def offset(index, bits):
    return sum(bit for at, bit in enumerate(bits) if index >> at & 1)


def index_of(distance, bits):
    index = 0
    for at, bit in enumerate(bits):
        index = index + ((distance >> (bit.bit_length() - 1)) & 1) * (1 << at)
    return index


def shard_index(shard, position, bits):
    if bits is None:
        return shard
    return index_of(shard ^ position, bits)


class Weights:
    def __init__(self, parts, refs, place):
        self.parts, self.refs = parts, refs
        self.section, self.position = place[0], place[1]

    def find(self, chunk):
        for number, (chunks, bits) in enumerate(self.parts):
            if chunk in chunks:
                return number, chunks.index(chunk), bits
        raise KeyError(chunk)

    def count(self, chunk):
        return self.refs[2 * self.find(chunk)[0]].shape[0]

    def shards(self, chunk):
        number, local, bits = self.find(chunk)
        ref = self.refs[2 * number]
        for shard in range(ref.shape[0]):
            yield shard, ref[shard_index(shard, self.position, bits), local]

    def pieces(self, chunk):
        number, local, bits = self.find(chunk)
        for ref, half in zip(self.refs[2 * number : 2 * number + 2], (self.section, 1 - self.section)):
            for shard in range(ref.shape[0]):
                yield shard, half, ref[shard_index(shard, self.position, bits), local]

    def square(self, target, row, column, chunk):
        for shard, half, value in self.pieces(chunk):
            piece, lanes = value.shape
            at = pl.ds(pl.multiple_of(column + half * lanes, lanes), lanes)
            target[row + shard * piece : row + (shard + 1) * piece, at] = value

    def wide(self, target, chunk):
        rows, width = target.shape
        for at in range(width // rows):
            self.square(target, 0, at * rows, chunk + at)

    def tall(self, target, chunk):
        count = target.shape[0] // target.shape[1]
        for step in range(count):
            for shard, half, value in self.pieces(chunk + step):
                piece, lanes = value.shape
                row = (shard * count + step) * piece
                target[row : row + piece, pl.ds(pl.multiple_of(half * lanes, lanes), lanes)] = value


def pack(stage, chunk, value):
    _, shards, _, piece, lanes = stage.shape
    for half in range(2):
        stage[half, :, chunk] = value[:, half * lanes : (half + 1) * lanes].reshape(shards, piece, lanes)


def pack_rows(stage, chunk, count, value):
    _, shards, _, piece, lanes = stage.shape
    for half in range(2):
        for shard in range(shards):
            for step in range(count):
                row = (shard * count + step) * piece
                stage[half, shard, chunk + step] = value[row : row + piece, half * lanes : (half + 1) * lanes]


def pack_wide(stage, chunk, value):
    rows, width = value.shape
    for at in range(width // rows):
        pack(stage, chunk + at, value[:, at * rows : (at + 1) * rows])


def pack_small(stage, chunk, mixing_vec, norm_vec, feed_vec, bias, up, vec, tile):
    _, shards, _, piece, lanes = stage.shape
    units = up.shape[1] // shards
    sources = (
        (mixing_vec, 0, 0, 1), (norm_vec, 0, 1, 1), (feed_vec, 0, 2, 1), (mixing_vec, 1, 3, 3),
        (norm_vec, 1, 6, 1), (bias, 0, 7, 2), (feed_vec, 1, 9, 3),
    )
    for ref, first, row, count in sources:
        vec[row : row + count, :] = ref[first : first + count, :]
    tile[...] = jnp.zeros(tile.shape, F32)
    for shard in range(shards):
        tile[:12, :piece] = vec[:12, shard * piece : (shard + 1) * piece]
        tile[12:13, :units] = up[:, shard * units : (shard + 1) * units]
        stage[0, shard, chunk] = tile[...].astype(BF16)
        stage[1, shard, chunk] = jnp.zeros((piece, lanes), BF16)


def hand_out(stage, place, outs, orders=None):
    section = place[0]
    if orders is None:
        outs[0][...] = stage[section]
        outs[1][...] = stage[1 - section]
        return
    for number, (first, count, bits) in enumerate(orders):
        for out, half in zip(outs[2 * number : 2 * number + 2], (section, 1 - section)):
            for index in range(out.shape[0]):
                shard = index if bits is None else place[1] ^ offset(index, bits)
                out[index] = stage[half, shard, first : first + count]


def vector(vec_ref, index):
    return vec_ref[index : index + 1, :]


def one_hot(condition):
    return condition.astype(F32).astype(BF16)


def slot_hot(place_row, slots):
    return one_hot(iota((slots, place_row.shape[1]), 0) == place_row[...])


def gather_hot(place_col, slots):
    return one_hot(iota((place_col.shape[0], slots), 1) == place_col[...])


def cut_shards(
    place, stencil, mixing, project_in, project_out, expand, reduce_w, keep_out, give_out
):
    kernel, piece, width = stencil.shape
    half = width // 2
    for out, which in ((keep_out, place[0]), (give_out, 1 - place[0])):
        start = pl.multiple_of(which * half, half)
        out[:kernel] = stencil[:, :, pl.ds(start, half)].astype(BF16)
        at = kernel
        for ref in (mixing, project_in, project_out, expand):
            for step in range(ref.shape[1] // width):
                out[at] = ref[:, pl.ds(pl.multiple_of(step * width + start, half), half)].astype(BF16)
                at += 1
        for step in range(reduce_w.shape[0] // piece):
            out[at] = reduce_w[step * piece : (step + 1) * piece, pl.ds(start, half)].astype(BF16)
            at += 1


def prepare(groups, capacity, target_row, target_col, cotangent, row_out, col_out, count_out, sent_out):
    rows = target_col.shape[0]
    earlier = one_hot(iota((rows, rows), 0) > iota((rows, rows), 1))
    later = one_hot(iota((rows, rows), 0) < iota((rows, rows), 1))
    for block in range(2):
        target = target_col[:, block : block + 1]
        hot = one_hot(iota((rows, groups), 1) == target)
        order = jnp.sum(dot(earlier, hot) * hot.astype(F32), axis=1, keepdims=True)
        col_out[:, block : block + 1] = target * capacity + order.astype(jnp.int32)
        count_out[block : block + 1, :] = column_sum(hot.astype(F32)).astype(jnp.int32)
        target = target_row[block : block + 1, :]
        hot = one_hot(iota((groups, rows), 0) == target)
        order = jnp.sum(dot(hot, later) * hot.astype(F32), axis=0, keepdims=True)
        row_out[block : block + 1, :] = target * capacity + order.astype(jnp.int32)
    hot = one_hot(iota((sent_out.shape[0], rows), 0) == row_out[1:2, :])
    sent_out[...] = dot(hot, cotangent[...]).astype(BF16)


def stencil_forward(parts, small_at, normed_sent, place, before, rows_in, after, near, place_row, *refs):
    if small_at is None:
        vectors_in, refs = refs[:3], refs[3:]
    halves, refs = refs[: 2 * len(parts)], refs[2 * len(parts) :]
    vec, up_bias, columns, padded, *refs = refs
    if normed_sent:
        first_out, cpe_out, sent_out, picked, weight, mixing = refs
    else:
        first_out, sent_out, picked, weight, mixing = refs
    rows, kernel = near.shape
    width = padded.shape[1]
    padded[:HALO, :] = before[...]
    padded[HALO : HALO + rows, :] = rows_in[...]
    padded[HALO + rows :, :] = after[...]
    chunk = 9
    weights = Weights(parts, halves, place)
    if small_at is None:
        vec[...], up_bias[...], columns[...] = (ref[...] for ref in vectors_in)
    else:
        for shard, value in weights.shards(small_at):
            piece, units = width // weights.count(small_at), up_bias.shape[1] // weights.count(small_at)
            value = value.astype(F32)
            vec[:, shard * piece : (shard + 1) * piece] = value[:12, :piece]
            up_bias[:, shard * units : (shard + 1) * units] = value[12:13, :units]
        wide = jnp.concatenate([vec[...], jnp.zeros((LANES - 12, width), F32)], axis=0).T
        columns[...] = wide[:, BIAS + 4 : BIAS + 6]
    for k in range(kernel):
        weights.square(weight, k * width, 0, k)
    weights.square(mixing, 0, 0, kernel)
    for block in range(rows // BLOCK):
        here = slice(block * BLOCK, (block + 1) * BLOCK)
        window = padded[block * BLOCK : block * BLOCK + WINDOW, :]
        lane = iota((BLOCK, WINDOW), 1) + block * BLOCK
        for low in range(0, kernel, chunk):
            ks = range(low, min(low + chunk, kernel))
            hot = jnp.concatenate([one_hot(near[here, k : k + 1] == lane) for k in ks], axis=0)
            got = dot(hot, window).astype(BF16)
            for at, k in enumerate(ks):
                picked[here, k * width : (k + 1) * width] = got[at * BLOCK : (at + 1) * BLOCK, :]
    first_low = (dot(picked[...], weight[...]) + vector(vec, BIAS)).astype(BF16)
    first_out[...] = first_low
    second = dot(first_low, mixing[...]) + vector(vec, BIAS + 1)
    inputs = padded[HALO : HALO + rows, :].astype(F32)
    cpe = inputs + norm(second, vector(vec, GAIN), vector(vec, BIAS + 2))
    if normed_sent:
        cpe_out[...] = cpe
        cpe = norm(cpe, vector(vec, GAIN + 1), vector(vec, BIAS + 3))
    sent_out[...] = dot(slot_hot(place_row, sent_out.shape[0]), cpe.astype(BF16)).astype(BF16)


def high_low(value):
    high = value.astype(BF16)
    return high, (value - high.astype(F32)).astype(BF16)


def of_head(group, head, size):
    return jnp.where(iota(group.shape, 1) // size == head % (LANES // size), group, jnp.zeros((), group.dtype))


def group_lanes(head, size):
    return pl.ds(pl.multiple_of(head * size // LANES * LANES, LANES), LANES)


def spread_heads(target, wide, narrow, ones):
    size = wide[0].shape[1] // HEADS
    sources = (*wide, *narrow)
    row, lane = iota((len(sources) * LANES, LANES), 0), iota((len(sources) * LANES, LANES), 1)
    first = len(wide) * size
    extra = ((iota((1, LANES), 1) >= first + len(narrow)) & (iota((1, LANES), 1) < first + len(narrow) + ones)).astype(F32)
    for head in range(HEADS):
        at, inner = (head * size) // LANES * LANES, (head * size) % LANES
        move = (lane < first) & (row == inner + lane % size + LANES * (lane // size))
        for number in range(len(narrow)):
            move = move | ((lane == first + number) & (row == inner + LANES * (len(wide) + number)))
        both = jnp.concatenate([source[:, at : at + LANES] for source in sources], axis=1)
        target[:, head * LANES : (head + 1) * LANES] = (dot(both, one_hot(move)) + extra).astype(BF16)


def project(patch, weight, vec, query_all, queries, key_all, key_rows, value_rows):
    width = patch.shape[1]
    query = (dot(patch, weight[:, :width]) + vector(vec, BIAS + 4)).astype(BF16)
    if query_all is not None:
        query_all[...] = query.T
    if queries is not None:
        high, low = high_low(query.astype(F32) * ((width // HEADS) ** -0.5 * LOG2E))
        spread_heads(queries, (high, low), (), 1)
    key_rows[...] = dot(patch, weight[:, width : 2 * width]).astype(BF16)
    if key_all is not None:
        key_all[...] = key_rows[...].T
    value_rows[...] = (dot(patch, weight[:, 2 * width :]) + vector(vec, BIAS + 5)).astype(BF16)


def four_powers(source, target, sems, four):
    count = source.shape[0] // (HEADS // 4)
    rows = pl.ds(pl.multiple_of(four * count, count), count)
    return pltpu.make_async_copy(source.at[rows], target.at[rows], sems.at[four])


def attend(queries, key_all, value_rows, mask_row, key, out, inverse_out, powers, powers_out=None, sems=None):
    slots, width = out.shape
    size = width // HEADS
    key[...] = jnp.zeros(key.shape, BF16)
    key[2 * size : 3 * size, :] = jnp.where(iota((size, slots), 0) == 0, mask_row, 0.0).astype(BF16)

    def one_head(shifted, head, carry):
        least, most = carry
        here = pl.ds(pl.multiple_of(head * size, size), size)
        key[:size, :] = key_all[here, :]
        key[size : 2 * size, :] = key_all[here, :]
        lanes, group = pl.ds(pl.multiple_of(head * LANES, LANES), LANES), group_lanes(head, size)
        value = jnp.concatenate([of_head(value_rows[:, group], head, size), jnp.ones((slots, LANES), BF16)], axis=1)
        for start in range(0, slots, STEP):
            part = slice(start, start + STEP)
            scores = dot(queries[part, lanes], key[...])
            if shifted:
                scores = scores - jnp.max(scores, axis=1, keepdims=True)
            power = jnp.exp2(scores).astype(BF16)
            powers[pl.ds(pl.multiple_of(head * slots + start, STEP), STEP), :] = power
            both = dot(power, value)
            total = both[:, LANES:]
            least = jnp.minimum(least, jnp.min(total, axis=0, keepdims=True))
            most = jnp.maximum(most, jnp.max(total, axis=0, keepdims=True))
            inverse = 1.0 / total
            out[part, group] += both[:, :LANES] * inverse
            inverse_out[part, group] += of_head(inverse, head, size)
        return least, most

    def four_heads(four, carry):
        carry = functools.reduce(lambda state, at: one_head(False, 4 * four + at, state), range(4), carry)
        if powers_out is not None:
            four_powers(powers, powers_out, sems, four).start()
        return carry

    def clear():
        out[...] = jnp.zeros(out.shape, F32)
        inverse_out[...] = jnp.zeros(inverse_out.shape, F32)

    clear()
    start = (jnp.full((1, LANES), 1.0, F32), jnp.full((1, LANES), 1.0, F32))
    least, most = lax.fori_loop(0, HEADS // 4, four_heads, start)
    if powers_out is not None:
        for four in range(HEADS // 4):
            four_powers(powers, powers_out, sems, four).wait()

    @pl.when(jnp.logical_not((jnp.min(least) > 2.0**-60) & (jnp.max(most) < 2.0**60)))
    def _():
        clear()
        lax.fori_loop(0, HEADS, functools.partial(one_head, True), start)
        if powers_out is not None:
            for four in range(HEADS // 4):
                four_powers(powers, powers_out, sems, four).start()
            for four in range(HEADS // 4):
                four_powers(powers, powers_out, sems, four).wait()


def attend_back(
    grad_rows, out, inverse, query_all, key_rows, value_rows, grads, value_all, grad_all, powers, value,
    grad_query, grad_key, grad_value, powers_in=None, sems=None,
):
    slots, width = out.shape
    size = width // HEADS
    grad_full, scale = grad_rows[...].astype(F32), inverse[...]
    high, low = high_low(grad_full * scale)
    same = one_hot(iota((width, width), 0) // size == iota((width, width), 1) // size)
    inner_high, inner_low = high_low(grad_full * out[...])
    less_high, less_low = high_low(-(dot(inner_high, same) + dot(inner_low, same)) * scale)
    spread_heads(grads, (high, low), (less_high, less_low), 0)
    grad_all[...] = high.T
    value_all[...] = value_rows[...].T
    value[...] = jnp.zeros(value.shape, BF16)
    value[2 * size : 3 * size, :] = one_hot(iota((size, slots), 0) < 2)
    grad_query[...] = jnp.zeros(grad_query.shape, F32)

    def one_head(head):
        here = pl.ds(pl.multiple_of(head * size, size), size)
        value[:size, :] = value_all[here, :]
        value[size : 2 * size, :] = value_all[here, :]
        lanes, group = pl.ds(pl.multiple_of(head * LANES, LANES), LANES), group_lanes(head, size)
        key_head = of_head(key_rows[:, group], head, size)
        query_head, grad_head = query_all[here, :], grad_all[here, :]
        toward_key = jnp.zeros((size, slots), F32)
        toward_value = jnp.zeros((size, slots), F32)
        for start in range(0, slots, STEP):
            part = slice(start, start + STEP)
            power = powers[pl.ds(pl.multiple_of(head * slots + start, STEP), STEP), :]
            change = (power.astype(F32) * dot(grads[part, lanes], value[...])).astype(BF16)
            toward_value += dot(grad_head[:, part], power)
            toward_key += dot(query_head[:, part], change)
            grad_query[part, group] += dot(change, key_head) * size**-0.5
        grad_key[here, :] = toward_key * size**-0.5
        grad_value[here, :] = toward_value

    def four_heads(four, carry):
        if powers_in is not None:
            four_powers(powers_in, powers, sems, four).wait()
        for at in range(4):
            one_head(4 * four + at)
        return carry

    lax.fori_loop(0, HEADS // 4, four_heads, 0)


def attention_forward(parts, chunk, place, patch_in, mask_row, vec, *refs):
    halves, refs = refs[: 2 * len(parts)], refs[2 * len(parts) :]
    low_out, out, inverse_out, powers_out, weight, queries, key_all, key_rows, value_rows, key, powers, sems = refs
    Weights(parts, halves, place).wide(weight, chunk)
    project(patch_in[...], weight, vec, None, queries, key_all, key_rows, value_rows)
    attend(queries, key_all, value_rows, mask_row[...], key, out, inverse_out, powers, powers_out, sems)
    low_out[...] = out[...].astype(BF16)


def attention_outputs(grad_query, grad_key, grad_value, patch, weight, grad_bias_out):
    grad_values = grad_value[...].T
    grad_bias_out[0:1, :] = column_sum(grad_query[...])
    grad_bias_out[1:2, :] = column_sum(grad_values)
    low_grads = jnp.concatenate([grad_query[...], grad_key[...].T, grad_values], axis=1).astype(BF16)
    return dot_tn(patch, low_grads).astype(BF16), dot_nt(low_grads, weight[...]).astype(BF16)


def attention_backward(parts, chunk, place, patch_in, grad_in, out_in, inverse_in, powers_in, vec, *refs):
    halves, refs = refs[: 2 * len(parts)], refs[2 * len(parts) :]
    grad_weight_out, grad_bias_out, grad_patch_out, *refs = refs
    weight, query_all, key_rows, value_rows, grads, value_all, grad_all, powers, value, *refs = refs
    grad_query, grad_key, grad_value, sems = refs
    for four in range(HEADS // 4):
        four_powers(powers_in, powers, sems, four).start()
    patch = patch_in[...]
    Weights(parts, halves, place).wide(weight, chunk)
    project(patch, weight, vec, query_all, None, None, key_rows, value_rows)
    attend_back(
        grad_in, out_in, inverse_in, query_all, key_rows, value_rows, grads, value_all, grad_all, powers, value,
        grad_query, grad_key, grad_value, powers_in, sems,
    )
    grad_weight_out[...], grad_patch_out[...] = attention_outputs(
        grad_query, grad_key, grad_value, patch, weight, grad_bias_out
    )


def unpack_feed(weights, chunk, project, expand, reduce_w):
    weights.wide(project, chunk)
    weights.wide(expand, chunk + 1)
    weights.tall(reduce_w, chunk + 1 + expand.shape[1] // expand.shape[0])


def feed_forward(parts, chunk, place, returned, place_col, cpe, vec, up_bias, *refs):
    halves, refs = refs[: 2 * len(parts)], refs[2 * len(parts) :]
    mixed_out, attn_out, low_out, first_out, last_out, project, expand, reduce_w = refs
    unpack_feed(Weights(parts, halves, place), chunk, project, expand, reduce_w)
    mixed = dot(gather_hot(place_col, returned.shape[0]), returned[...]).astype(BF16)
    mixed_out[...] = mixed
    attn = cpe[...] + dot(mixed, project[...]) + vector(vec, BIAS + 6)
    attn_out[...] = attn
    hidden = norm(attn, vector(vec, GAIN + 2), vector(vec, BIAS + 7)).astype(BF16)
    gated = gelu(dot(hidden, expand[...]) + up_bias[...]).astype(BF16)
    low = (attn + dot(gated, reduce_w[...]) + vector(vec, BIAS + 8)).astype(BF16)
    low_out[...] = low
    first_out[...] = low[:HALO, :]
    last_out[...] = low[-HALO:, :]


def feed_back(mixed, attn, grad_low, project, expand, reduce_w, vec, up_bias, stage, chunk, grad_vec_out, grad_up_out):
    unit, scale = norm_parts(attn)
    hidden = (unit * vector(vec, GAIN + 2) + vector(vec, BIAS + 7)).astype(BF16)
    gated_full, slope = gelu_parts(dot(hidden, expand[...]) + up_bias[...])
    gated = gated_full.astype(BF16)
    grad_full = grad_low.astype(F32)
    grad_up = dot_nt(grad_low, reduce_w[...]) * slope
    grad_up_out[...] = column_sum(grad_up)
    grad_up_low = grad_up.astype(BF16)
    grad_rows, grad_gain, grad_shift = norm_back(
        unit, scale, vector(vec, GAIN + 2), dot_nt(grad_up_low, expand[...])
    )
    grad_attn = grad_full + grad_rows
    grad_attn_low = grad_attn.astype(BF16)
    grad_mixed = dot_nt(grad_attn_low, project[...]).astype(BF16)
    count = expand.shape[1] // expand.shape[0]
    pack_wide(stage, chunk, dot_tn(mixed, grad_attn_low).astype(BF16))
    pack_wide(stage, chunk + 1, dot_tn(hidden, grad_up_low).astype(BF16))
    pack_rows(stage, chunk + 1 + count, count, dot_tn(gated, grad_low).astype(BF16))
    grad_vec_out[0:1, :] = grad_gain
    grad_vec_out[1:2, :] = column_sum(grad_attn)
    grad_vec_out[2:3, :] = grad_shift
    grad_vec_out[3:4, :] = column_sum(grad_full)
    return gated, grad_attn, grad_mixed


def feed_backward(
    parts, chunk, place, mixed, attn, grad_cpe, own, before, after, place_row, vec, up_bias, *refs
):
    halves, refs = refs[: 2 * len(parts)], refs[2 * len(parts) :]
    keep_out, give_out, grad_attn_out, sent_out, grad_vec_out, grad_up_out, project, expand, reduce_w, stage, whole = refs
    whole[...] = own[...]
    whole[:HALO, :] += before[...].astype(F32)
    whole[-HALO:, :] += after[...].astype(F32)
    grad_low = (grad_cpe[...] + whole[...].astype(BF16).astype(F32)).astype(BF16)
    unpack_feed(Weights(parts, halves, place), chunk, project, expand, reduce_w)
    _, grad_attn_out[...], grad_mixed = feed_back(
        mixed[...], attn[...], grad_low, project, expand, reduce_w, vec, up_bias, stage, 0, grad_vec_out, grad_up_out
    )
    sent_out[...] = dot(slot_hot(place_row, sent_out.shape[0]), grad_mixed).astype(BF16)
    hand_out(stage, place, (keep_out, give_out))


def turn_around(parts, chunk, place, patch_in, grad_in, mask, mask_row, vec, up_bias, *refs):
    halves, refs = refs[: 2 * len(parts)], refs[2 * len(parts) :]
    keep_out, give_out, grad_bias_out, grad_patch_out, output_out, grad_vec_out, grad_norm_out, grad_up_out, *refs = refs
    weight, project_out, expand, reduce_w, queries, query_all, key_all, key_rows, value_rows, *refs = refs
    grads, value_all, grad_all, key, out, inverse, powers, grad_query, grad_key, grad_value, stage = refs
    weights = Weights(parts, halves, place)
    weights.wide(weight, chunk)
    unpack_feed(weights, chunk + 3, project_out, expand, reduce_w)
    slots, width = patch_in.shape
    grad_low = grad_in[...]
    rows = patch_in[...].astype(F32)
    unit, scale = norm_parts(rows)
    normed = unit * vector(vec, GAIN + 1) + vector(vec, BIAS + 3)
    patch = jnp.where(mask[...] < 0.0, 0.0, normed).astype(BF16)
    project(patch, weight, vec, query_all, queries, key_all, key_rows, value_rows)
    attend(queries, key_all, value_rows, mask_row[...], key, out, inverse, powers)
    mixed = out[...].astype(BF16)
    attn = rows + dot(mixed, project_out[...]) + vector(vec, BIAS + 6)
    gated, grad_attn, grad_mixed = feed_back(
        mixed, attn, grad_low, project_out, expand, reduce_w, vec, up_bias, stage, 3, grad_vec_out, grad_up_out
    )
    output_out[...] = (attn + dot(gated, reduce_w[...]) + vector(vec, BIAS + 8)).astype(BF16)
    attend_back(
        grad_mixed, out, inverse, query_all, key_rows, value_rows, grads, value_all, grad_all, powers, key,
        grad_query, grad_key, grad_value,
    )
    grad_weight, grad_patch = attention_outputs(grad_query, grad_key, grad_value, patch, weight, grad_bias_out)
    pack_wide(stage, 0, grad_weight)
    hand_out(stage, place, (keep_out, give_out))
    grad_normed = grad_patch.astype(F32)
    unit, scale = norm_parts(rows)
    grad_rows, grad_gain, grad_shift = norm_back(unit, scale, vector(vec, GAIN + 1), grad_normed)
    grad_norm_out[0:1, :] = grad_gain
    grad_norm_out[1:2, :] = grad_shift
    grad_patch_out[...] = (grad_attn + grad_rows).astype(BF16)


def collect(returned, place_col, out):
    out[...] = dot(gather_hot(place_col, returned.shape[0]), returned[...])


def mixing_back(grad_cpe, first, mixing, vec, grad_vec_out):
    first_low = first[...]
    second = dot(first_low, mixing[...]) + vector(vec, BIAS + 1)
    unit, scale = norm_parts(second)
    grad_second, grad_gain, grad_shift = norm_back(unit, scale, vector(vec, GAIN), grad_cpe)
    grad_second_low = grad_second.astype(BF16)
    grad_first = dot_nt(grad_second_low, mixing[...])
    grad_vec_out[0:1, :] = grad_gain
    grad_vec_out[1:2, :] = column_sum(grad_first)
    grad_vec_out[2:3, :] = column_sum(grad_second)
    grad_vec_out[3:4, :] = grad_shift
    return grad_first.astype(BF16), dot_tn(first_low, grad_second_low).astype(BF16)


def stencil_weights_back(padded, near_row, grad_first, stage, picked):
    kernel, rows = near_row.shape
    width = padded.shape[1]
    for block in range(rows // BLOCK):
        here = slice(block * BLOCK, (block + 1) * BLOCK)
        window = padded[block * BLOCK : block * BLOCK + WINDOW, :].T
        row = iota((WINDOW, BLOCK), 0) + block * BLOCK
        for low in range(0, kernel, 2):
            ks = range(low, min(low + 2, kernel))
            hot = jnp.concatenate([one_hot(near_row[k : k + 1, here] == row) for k in ks], axis=1)
            got = dot(window, hot).astype(BF16)
            for at, k in enumerate(ks):
                picked[k * width : (k + 1) * width, here] = got[:, at * BLOCK : (at + 1) * BLOCK]
    step = 3
    for low in range(0, kernel, step):
        got = dot(picked[low * width : (low + step) * width, :], grad_first).astype(BF16)
        for k in range(low, min(low + step, kernel)):
            pack(stage, k, got[(k - low) * width : (k - low + 1) * width, :])


def stencil_inputs_back(near_row, grad_first, weight, own_out, ahead_out, behind_out, toward, total):
    kernel, rows = near_row.shape
    width = weight.shape[1]
    for k in range(kernel):
        toward[k] = dot_nt(grad_first, weight[k * width : (k + 1) * width, :]).astype(BF16)
    total[...] = jnp.zeros(total.shape, F32)
    for block in range(rows // BLOCK):
        here = slice(block * BLOCK, (block + 1) * BLOCK)
        row = iota((WINDOW, BLOCK), 0) + block * BLOCK
        gathered = jnp.zeros((WINDOW, width), F32)
        for low in range(0, kernel, 2):
            ks = range(low, min(low + 2, kernel))
            hot = jnp.concatenate([one_hot(near_row[k : k + 1, here] == row) for k in ks], axis=1)
            gathered += dot(hot, jnp.concatenate([toward[k, here, :] for k in ks], axis=0))
        total[block * BLOCK : block * BLOCK + WINDOW, :] += gathered
    own_out[...] = total[HALO : HALO + rows, :]
    ahead_out[...] = total[:HALO, :].astype(BF16)
    behind_out[...] = total[HALO + rows :, :].astype(BF16)


def unpack_stencil(weights, weight):
    width = weight.shape[1]
    for k in range(weight.shape[0] // width):
        weights.square(weight, k * width, 0, k)


def last_inputs_back(parts, place, returned, place_col, first, near_row, vec, *refs):
    halves, refs = refs[: 2 * len(parts)], refs[2 * len(parts) :]
    grad_cpe_out, own_out, ahead_out, behind_out, grad_first_out, grad_mixing_out, grad_vec_out, *refs = refs
    weight, mixing, toward, total = refs
    weights = Weights(parts, halves, place)
    unpack_stencil(weights, weight)
    weights.square(mixing, 0, 0, near_row.shape[0])
    grad_cpe = dot(gather_hot(place_col, returned.shape[0]), returned[...])
    grad_cpe_out[...] = grad_cpe
    grad_first, grad_mixing_out[...] = mixing_back(grad_cpe, first, mixing, vec, grad_vec_out)
    grad_first_out[...] = grad_first
    stencil_inputs_back(near_row, grad_first, weight, own_out, ahead_out, behind_out, toward, total)


def last_gradients(
    bits, in_at, place, padded, near_row, grad_first, grad_mixing, rest_keep, rest_give, feed_keep, feed_give,
    mixing_vec, norm_vec, feed_vec, bias, up, keep_out, give_out, picked, stage, vec, tile,
):
    stencil_weights_back(padded, near_row, grad_first[...], stage, picked)
    pack(stage, in_at - 1, grad_mixing[...])
    pack_small(stage, in_at, mixing_vec, norm_vec, feed_vec, bias, up, vec, tile)
    section, position = place[0], place[1]
    last = in_at + rest_keep.shape[1]
    for out, half, rest, feed in (
        (keep_out, section, rest_keep, feed_keep),
        (give_out, 1 - section, rest_give, feed_give),
    ):
        for near in range(NEAR):
            for index in range(out.shape[1]):
                shard = ((position // NEAR) ^ (offset(index, bits) // NEAR)) * NEAR + near
                out[near, index, :in_at] = stage[half, shard, :in_at]
                out[near, index, in_at:last] = rest[shard]
                out[near, index, last : last + 1] = stage[half, shard, in_at:]
                out[near, index, last + 1 :] = feed[shard]


def first_gradients(
    parts, orders, in_at, place, returned, place_col, grad_attn, cpe, first, padded, near_row, vec, grad_in,
    feed_vec, bias, up, *refs
):
    halves, refs = refs[: 2 * len(parts)], refs[2 * len(parts) :]
    outs, refs = refs[: 2 * len(orders)], refs[2 * len(orders) :]
    grad_cpe_out, grad_first_out, mixing, picked, stage, mixing_vec, norm_vec, rows, tile = refs
    grad_first, grad_mixing = normed_back(
        parts, halves, place, returned, place_col, grad_attn, cpe, first, near_row.shape[0], vec, mixing,
        grad_cpe_out, grad_first_out, mixing_vec, norm_vec,
    )
    stencil_weights_back(padded, near_row, grad_first, stage, picked)
    pack(stage, in_at - 1, grad_mixing)
    pack_wide(stage, in_at, grad_in[...])
    out_at = in_at + 3
    pack_small(stage, out_at, mixing_vec, norm_vec, feed_vec, bias, up, rows, tile)
    section, position = place[0], place[1]
    for number, (start, count, bits) in enumerate(orders):
        for out, half in zip(outs[2 * number : 2 * number + 2], (section, 1 - section)):
            for index in range(out.shape[0]):
                out[index] = stage[half, position ^ offset(index, bits), start : start + count]


def last_weights_back(place, padded, near_row, grad_first, grad_mixing, keep_out, give_out, picked, stage):
    stencil_weights_back(padded, near_row, grad_first[...], stage, picked)
    pack(stage, near_row.shape[0], grad_mixing[...])
    hand_out(stage, place, (keep_out, give_out))


def normed_back(
    parts, halves, place, returned, place_col, grad_attn, cpe, first, mixing_at, vec, mixing,
    grad_cpe_out, grad_first_out, grad_vec_out, grad_norm_out,
):
    Weights(parts, halves, place).square(mixing, 0, 0, mixing_at)
    grad_normed = dot(gather_hot(place_col, returned.shape[0]), returned[...])
    unit, scale = norm_parts(cpe[...])
    back, grad_gain, grad_shift = norm_back(unit, scale, vector(vec, GAIN + 1), grad_normed)
    grad_norm_out[0:1, :] = grad_gain
    grad_norm_out[1:2, :] = grad_shift
    grad_cpe = grad_attn[...] + back
    grad_cpe_out[...] = grad_cpe
    grad_first, grad_mixing = mixing_back(grad_cpe, first, mixing, vec, grad_vec_out)
    grad_first_out[...] = grad_first
    return grad_first, grad_mixing


def first_weights_back(
    parts, orders, place, returned, place_col, grad_attn, cpe, first, padded, near_row, vec, grad_in, *refs
):
    halves, refs = refs[: 2 * len(parts)], refs[2 * len(parts) :]
    outs, refs = refs[: 2 * len(orders)], refs[2 * len(orders) :]
    grad_cpe_out, grad_first_out, grad_vec_out, grad_norm_out, mixing, picked, stage = refs
    grad_first, grad_mixing = normed_back(
        parts, halves, place, returned, place_col, grad_attn, cpe, first, near_row.shape[0], vec, mixing,
        grad_cpe_out, grad_first_out, grad_vec_out, grad_norm_out,
    )
    stencil_weights_back(padded, near_row, grad_first, stage, picked)
    pack(stage, near_row.shape[0], grad_mixing)
    pack_wide(stage, near_row.shape[0] + 1, grad_in[...])
    hand_out(stage, place, outs, orders)


def finish(place, kept, other, stencil_out, mixing_out, in_out, out_out, expand_out, reduce_out, small_out):
    section = place[0]
    chunks, piece, half = kept.shape
    kernel = stencil_out.shape[0]
    width = 2 * half
    for ref, which in ((kept, section), (other, 1 - section)):
        start = pl.multiple_of(which * half, half)
        stencil_out[:, :, pl.ds(start, half)] = ref[:kernel].astype(F32)
        at = kernel
        for out in (mixing_out, in_out, out_out, expand_out):
            for step in range(out.shape[1] // width):
                out[:, pl.ds(pl.multiple_of(step * width + start, half), half)] = ref[at].astype(F32)
                at += 1
        for step in range(reduce_out.shape[0] // piece):
            reduce_out[step * piece : (step + 1) * piece, pl.ds(start, half)] = ref[at].astype(F32)
            at += 1

    def small(ref):
        small_out[...] = ref[chunks - 1].astype(F32)

    @pl.when(section == 0)
    def _():
        small(kept)

    @pl.when(section == 1)
    def _():
        small(other)


def first_inputs_back(parts, place, near_row, grad_first, *refs):
    halves, refs = refs[: 2 * len(parts)], refs[2 * len(parts) :]
    own_out, ahead_out, behind_out, weight, toward, total = refs
    unpack_stencil(Weights(parts, halves, place), weight)
    stencil_inputs_back(near_row, grad_first[...], weight, own_out, ahead_out, behind_out, toward, total)


class Window:
    def __init__(self, array, first, count):
        self.array, self.first, self.count = array, first, count

    def scratch(self):
        shards, _, piece, lanes = self.array.shape
        return pltpu.VMEM((shards, self.count, piece, lanes), self.array.dtype)


class Outside(jax.ShapeDtypeStruct):
    pass


def call(body, name, outs, args, scratch=(), outside=()):
    windows = [(at, a) for at, a in enumerate(args) if isinstance(a, Window)]
    arrays = [a.array if isinstance(a, Window) else a for a in args]
    spaces = [
        pltpu.SMEM
        if a.shape == (2,)
        else pltpu.HBM
        if isinstance(window, Window)
        else pl.ANY
        if at in outside
        else pltpu.VMEM
        for at, (a, window) in enumerate(zip(arrays, args))
    ]

    def with_windows(*refs):
        refs, copied, sems = list(refs[: -len(windows) - 1]), refs[-len(windows) - 1 : -1], refs[-1]
        copies = []
        for number, (at, window) in enumerate(windows):
            source = refs[at].at[:, window.first : window.first + window.count]
            copies.append(pltpu.make_async_copy(source, copied[number], sems.at[number]))
            copies[-1].start()
            refs[at] = copied[number]
        for copy in copies:
            copy.wait()
        body(*refs)

    extra = [window.scratch() for _, window in windows] + [pltpu.SemaphoreType.DMA((len(windows),))] * bool(windows)
    return pl.pallas_call(
        with_windows if windows else body,
        out_shape=tuple(jax.ShapeDtypeStruct(o.shape, o.dtype) for o in outs),
        in_specs=[pl.BlockSpec(memory_space=space) for space in spaces],
        out_specs=tuple(pl.BlockSpec(memory_space=pl.ANY if isinstance(o, Outside) else pltpu.VMEM) for o in outs),
        scratch_shapes=[*scratch, *extra],
        compiler_params=pltpu.CompilerParams(vmem_limit_bytes=56 * 1024 * 1024),
        cost_estimate=pl.CostEstimate(flops=1, bytes_accessed=1, transcendentals=0),
        name=name,
    )(*arrays)


def like(*shape, dtype=F32):
    return jax.ShapeDtypeStruct(shape, dtype)


def low_like(*shape):
    return jax.ShapeDtypeStruct(shape, BF16)


def swap(value):
    return lax.ppermute(value, "section", [(0, 1), (1, 0)])


def neighbours_along(axis):
    count = lax.axis_size(axis)
    up = [(i, i + 1) for i in range(count - 1)]
    return up, [(j, i) for i, j in up]


def beside(first, last):
    up, down = neighbours_along(POINTS)
    return lax.ppermute(last, POINTS, up), lax.ppermute(first, POINTS, down)


def exchange(pieces):
    return lax.all_to_all(pieces, POINTS, split_axis=0, concat_axis=0, tiled=True)


def to_all(value, groups):
    slots, width = value.shape
    return exchange(value.reshape(groups, slots // groups, width)).reshape(slots, width)


def shards(
    boundary,
    stencil_weight,
    mixing_weight,
    project_in,
    project_out,
    expand_weight,
    reduce_weight,
    norm_gains,
    bias_rows,
    expand_bias,
    patch_index,
    neighbors,
):
    section = lax.axis_index("section")
    groups = lax.axis_size(POINTS)
    position = lax.axis_index(POINTS)
    rows, width = boundary.shape[2:]
    kernel = stencil_weight.shape[1]
    units = expand_weight.shape[2]
    capacity = max(2, 3 * rows // (2 * groups))
    slots = groups * capacity
    size = width // HEADS
    piece = width // groups
    half = width // 2
    ups = units // width
    front_chunks, rest_chunks = kernel + 1, 4 + 2 * ups
    at_first = section == 0
    place = jnp.stack([section, position]).astype(jnp.int32)
    direct = piece % 16 == 0
    chunks = kernel + 6 + 2 * ups
    mixing_at, in_at, out_at, small_at = kernel, kernel + 1, kernel + 4, chunks - 1
    feeds = range(out_at, small_at)
    far = [groups >> at for at in range(1, groups.bit_length())]
    near_last = (far, far[:-2] + far[:-3:-1])

    def of_section(value, which):
        return lax.dynamic_index_in_dim(value, which, 0, keepdims=False)

    def together(*values):
        return lax.optimization_barrier(values)

    def chunks_of(shard):
        return shard.reshape(-1, shard.shape[-1] // width, width).transpose(1, 0, 2).reshape(-1, piece, width)

    if direct:
        own_half, other_half = call(
            cut_shards,
            "cut_shards",
            (low_like(small_at, piece, half), low_like(small_at, piece, half)),
            (
                place,
                stencil_weight[0],
                mixing_weight[0],
                project_in[0],
                project_out[0],
                expand_weight[0],
                reduce_weight[0],
            ),
        )
    else:
        shard = jnp.concatenate(
            [
                stencil_weight[0],
                mixing_weight,
                chunks_of(project_in[0]),
                project_out,
                chunks_of(expand_weight[0]),
                reduce_weight[0].reshape(ups, piece, width),
            ],
            axis=0,
        ).astype(BF16)

        def lanes(value, which):
            return lax.dynamic_slice_in_dim(value, which * half, half, axis=value.ndim - 1)

        own_half, other_half = lanes(shard, section), lanes(shard, 1 - section)
    other_half = swap(other_half)
    halves = (jnp.where(at_first, own_half, other_half), jnp.where(at_first, other_half, own_half))
    halves, boundary, patch_index, neighbors, norm_gains, bias_rows, expand_bias = together(
        halves, boundary, patch_index, neighbors, norm_gains, bias_rows, expand_bias
    )
    if direct:
        small = jnp.concatenate([norm_gains[0], bias_rows[0]], axis=0)
        small = jnp.concatenate(
            [
                jnp.pad(small, ((0, 0), (0, half - piece))),
                jnp.pad(expand_bias, ((0, piece - 13), (0, half - units // groups))),
            ],
            axis=0,
        ).astype(BF16)
    else:
        small = jnp.concatenate([norm_gains[0].reshape(-1), bias_rows[0].reshape(-1), expand_bias[0]])
        small = jnp.pad(small, (0, piece * half - small.shape[0])).reshape(piece, half).astype(BF16)
    other_small = swap(small)
    smalls = (jnp.where(at_first, small, other_small), jnp.where(at_first, other_small, small))

    def partner(value, distance):
        return lax.ppermute(value, POINTS, [(i, i ^ distance) for i in range(groups)])

    def doubled(value, distances):
        for distance in distances:
            value = jnp.concatenate([value, partner(value, distance)], axis=0)
        return value

    def halved(value, distances):
        for distance in distances[::-1]:
            middle = value.shape[0] // 2
            value = (value[:middle].astype(F32) + partner(value[middle:], distance).astype(F32)).astype(BF16)
        return value

    def in_device_order(value, bits):
        return value[shard_index(jnp.arange(groups, dtype=jnp.int32), position, bits)]

    def as_squares(value, numbers):
        tall = len([number for number in numbers if number >= small_at - ups])
        first = len(numbers) - tall
        pieces = [value[:, :first].transpose(1, 0, 2, 3).reshape(first, width, half)]
        if tall:
            pieces.append(value[:, first : first + tall].reshape(tall, width, half))
        return jnp.concatenate(pieces, axis=0)[None]

    def part_of(gathered, numbers, bits):
        numbers = tuple(numbers)
        if not direct:
            numbers = tuple(number for number in numbers if number < small_at)
            gathered = as_squares(gathered if bits is None else in_device_order(gathered, bits), numbers)
            bits = None
        return (gathered, swap(gathered)), (numbers, bits)

    vectors = 12 * piece
    small_part = small_at if direct else None
    vector_likes = (like(12, width), like(1, units), like(width, 2))
    padded_like = low_like(rows + 2 * HALO, width)

    def vectors_of(shards_small):
        if direct:
            return ()
        values = shards_small.reshape(groups, -1)
        vec, up = values[:, :vectors].astype(F32).reshape(groups, 12, piece), values[:, vectors : vectors + units // groups]
        vec = vec.transpose(1, 0, 2).reshape(12, width)
        return vec, up.astype(F32).reshape(1, units), jnp.stack([vec[BIAS + 4], vec[BIAS + 5]], axis=1)

    stage_shape = (groups, piece) if direct else (1, width)

    def stage_like(number):
        return low_like(stage_shape[0], number, stage_shape[1], half)

    def stage_scratch(number):
        return pltpu.VMEM((2, stage_shape[0], number, stage_shape[1], half), BF16)

    def as_shards(value, tall=0):
        if direct:
            return value
        first = value.shape[1] - tall
        main = value[0, :first].reshape(first, groups, piece, half).transpose(1, 0, 2, 3)
        return jnp.concatenate([main, value[0, first:].reshape(groups, tall, piece, half)], axis=1)

    def small_chunk(mixing_vec, norm_vec, feed_vec, bias, up):
        vec = jnp.concatenate(
            [mixing_vec[0:1], norm_vec[0:1], feed_vec[0:1], mixing_vec[1:4], norm_vec[1:2], bias, feed_vec[1:4]],
            axis=0,
        )
        vec = vec.reshape(12, groups, piece).transpose(1, 0, 2).reshape(groups, vectors)
        vec = jnp.concatenate([vec, up.reshape(groups, units // groups)], axis=1)
        vec = jnp.pad(vec, ((0, 0), (0, piece * half - vec.shape[1]))).reshape(groups, 1, piece, half).astype(BF16)
        none = jnp.zeros_like(vec)
        return jnp.where(at_first, vec, none), jnp.where(at_first, none, vec)

    def across(keep, give):
        return (keep.astype(F32) + swap(give).astype(F32)).astype(BF16)

    mine = of_section(boundary[0], section)
    theirs = swap(of_section(boundary[0], 1 - section))
    inputs = jnp.where(at_first, mine, theirs)
    cotangent = jnp.where(at_first, theirs, mine)
    index = patch_index[0, :, :, 0]
    own_index = of_section(index, section)
    other_index = swap(of_section(index, 1 - section))
    targets = jnp.stack([jnp.where(at_first, own_index, other_index), jnp.where(at_first, other_index, own_index)])
    linked = of_section(neighbors, section)
    near = jnp.where(linked >= 0, linked - position * rows + HALO, ABSENT)
    near_row = near.T
    place_rows, place_cols, counts, cotangent_sent = call(
        functools.partial(prepare, groups, capacity),
        "prepare",
        (
            like(2, rows, dtype=jnp.int32),
            like(rows, 2, dtype=jnp.int32),
            like(2, groups, dtype=jnp.int32),
            low_like(slots, width),
        ),
        (targets, targets.T, cotangent),
    )
    numbers = jnp.pad(counts.reshape(1, 2 * groups).astype(BF16), ((0, piece - 1), (0, half - 2 * groups)))
    windows = ((0, kernel, 1), (out_at, small_at, 0), (in_at, small_at, 1), (mixing_at, in_at, 1))
    spread = jnp.concatenate([halves[block][first:last] for first, last, block in windows], axis=0)
    spread = lax.all_gather(spread, POINTS, axis=0, tiled=False)

    picked = [*range(out_at), small_at, chunks, chunks + 1]
    middle = len(picked) // 2
    close = doubled(halves[0][None, :out_at], far[:-3])
    late = doubled(jnp.stack([*smalls, numbers])[None], far[:-3])
    close = doubled(jnp.concatenate([close, late], axis=1), far[-3:-2])
    close, near, near_row, inputs = together(close, near, near_row, inputs)
    halo0 = beside(inputs[:HALO], inputs[-HALO:])
    ends = [close[:, :middle], close[:, middle:]]
    rows_of = (place_rows[0:1], place_rows[1:2])
    cols_of = (place_cols[:, 0:1], place_cols[:, 1:2])
    ends = [doubled(end, distances[-2:]) for end, distances in zip(ends, near_last)]
    *halo0, end_a, end_b = together(*halo0, *ends)
    ends = [end_a, end_b]
    zbits = far[:-2]
    refs_a, part_a = part_of(ends[0], picked[:middle], near_last[0])
    refs_b, part_b = part_of(ends[1], picked[middle:], near_last[1])
    refs0, parts0 = (*refs_a, *refs_b), (part_a, part_b)
    vectors0 = vectors_of(in_device_order(ends[1][:, -3], near_last[1]))
    arrived = in_device_order(ends[1][:, -1, 0, : 2 * groups], near_last[1]).reshape(groups, 2, groups)
    arrived = lax.dynamic_index_in_dim(arrived, position, 2, keepdims=False).astype(jnp.int32)
    slot = jnp.arange(slots, dtype=jnp.int32)
    present = (slot % capacity)[:, None] < jnp.repeat(arrived, capacity, axis=0)
    masks = jnp.where(present, 0.0, NEGATIVE).astype(F32)
    mask_rows, masks = masks.T, (masks[:, 0:1], masks[:, 1:2])
    mask_rows = (mask_rows[0:1], mask_rows[1:2])


    def scratch(shape, dtype=BF16):
        return pltpu.VMEM(shape, dtype)

    stencil_scratch = [scratch((rows, kernel * width)), scratch((kernel * width, width)), scratch((width, width))]
    feed_scratch = [scratch((width, width)), scratch((width, units)), scratch((units, width))]
    lane_rows = scratch((slots, HEADS * LANES))
    tall_low = scratch((slots, width))
    tall, flat = scratch((slots, width), F32), scratch((width, slots), F32)
    wide_low = scratch((width, slots))
    head_rows = scratch((LANES, slots))

    vec0, up_bias0, columns0, padded0, first0, cpe0, sent = call(
        functools.partial(stencil_forward, parts0, small_part, True),
        "stencil_forward_0",
        (*vector_likes, padded_like, low_like(rows, width), like(rows, width), low_like(slots, width)),
        (place, halo0[0], inputs, halo0[1], near, rows_of[0], *vectors0, *refs0),
        stencil_scratch,
    )
    patch0 = to_all(sent, groups)
    patch0, cotangent_sent, spread, mask_rows, masks = together(patch0, cotangent_sent, spread, mask_rows, masks)
    cotangent_patch, other_spread = to_all(cotangent_sent, groups), swap(spread)
    powers_like = Outside((HEADS * slots, slots), BF16)
    powers = scratch(powers_like.shape)
    four_sems = pltpu.SemaphoreType.DMA((HEADS // 4,))
    out, rows0, inverse0, powers0 = call(
        functools.partial(attention_forward, parts0[1:], in_at),
        "attention_forward_0",
        (low_like(slots, width), like(slots, width), like(slots, width), powers_like),
        (place, patch0, mask_rows[0], vec0, *refs_b),
        [
            scratch((width, 3 * width)),
            lane_rows,
            wide_low,
            tall_low,
            tall_low,
            head_rows,
            powers,
            four_sems,
        ],
    )
    out, cotangent_patch, other_spread = together(out, cotangent_patch, other_spread)
    returned = to_all(out, groups)
    spread_parts, first = [], 0
    for low, high, block in windows:
        number = high - low
        if direct:
            refs = (Window(spread, first, number), Window(other_spread, first, number))
            spread_parts.append((refs, (tuple(range(low, high)), None)))
        else:
            spread_parts.append(part_of(spread[:, first : first + number], range(low, high), None))
        first += number
    (refs_s, part_s), (feed_refs0, feed_part0), (rest_refs1, rest_part1), (refs_m, part_m) = spread_parts
    refs1, parts1, feed_parts0, rest_parts1 = (*refs_s, *refs_m), (part_s, part_m), (feed_part0,), (rest_part1,)
    forward_refs1, forward_parts1 = refs1, parts1
    if direct:
        at = len(part_b[0]) - 2
        forward_refs1 = (*refs1, *(Window(ref, at, 1) for ref in refs_b))
        forward_parts1 = (*parts1, ((small_at,), near_last[1]))
    vectors1 = vectors_of(in_device_order(ends[1][:, -2], near_last[1]))
    mixed0, attn0, middle, middle_first, middle_last = call(
        functools.partial(feed_forward, feed_parts0, out_at),
        "feed_forward_0",
        (
            low_like(rows, width),
            like(rows, width),
            low_like(rows, width),
            low_like(HALO, width),
            low_like(HALO, width),
        ),
        (place, returned, cols_of[0], cpe0, vec0, up_bias0, *feed_refs0),
        feed_scratch,
    )

    before, after = beside(middle_first, middle_last)
    vec1, up_bias1, columns1, padded1, first1, sent = call(
        functools.partial(stencil_forward, forward_parts1, small_part, False),
        "stencil_forward_1",
        (*vector_likes, padded_like, low_like(rows, width), low_like(slots, width)),
        (place, before, middle, after, near, rows_of[1], *vectors1, *forward_refs1),
        stencil_scratch,
    )
    patch1 = to_all(sent, groups)
    rest_keep1, rest_give1, bias1, grad_patch, output_sent, feed_vec1, norm_vec1, up1 = call(
        functools.partial(turn_around, rest_parts1, in_at),
        "turn_around_1",
        (
            stage_like(3 + len(feeds)),
            stage_like(3 + len(feeds)),
            like(2, width),
            low_like(slots, width),
            low_like(slots, width),
            like(4, width),
            like(2, width),
            like(1, units),
        ),
        (place, patch1, cotangent_patch, masks[1], mask_rows[1], vec1, up_bias1, *rest_refs1),
        [
            scratch((width, 3 * width)),
            *feed_scratch,
            lane_rows,
            wide_low,
            wide_low,
            tall_low,
            tall_low,
            lane_rows,
            wide_low,
            wide_low,
            head_rows,
            tall,
            tall,
            powers,
            tall,
            flat,
            flat,
            stage_scratch(3 + len(feeds)),
        ],
    )
    returned = to_all(grad_patch, groups)

    returned, output_sent = together(returned, output_sent)
    output_back = to_all(output_sent, groups)
    stencil_back_scratch = [
        scratch((kernel * width, width)),
        scratch((kernel, rows, width)),
        scratch((rows + 2 * HALO, width), F32),
    ]
    grad_cpe, own, ahead, behind, grad_first, grad_mixing, mixing_vec1 = call(
        functools.partial(last_inputs_back, parts1),
        "stencil_inputs_1",
        (
            like(rows, width),
            like(rows, width),
            low_like(HALO, width),
            low_like(HALO, width),
            low_like(rows, width),
            low_like(width, width),
            like(4, width),
        ),
        (place, returned, cols_of[1], first1, near_row, vec1, *refs1),
        [stencil_back_scratch[0], scratch((width, width)), *stencil_back_scratch[1:]],
    )

    def with_rims(grad_cpe, own, from_before, from_after):
        empty = jnp.zeros((rows - 2 * HALO, width), F32)
        own = own + jnp.concatenate([from_before.astype(F32), empty, from_after.astype(F32)], axis=0)
        return grad_cpe + own.astype(BF16).astype(F32)

    ahead, output_back = together(ahead, output_back)
    from_before, from_after = beside(ahead, behind)

    feed_keep0, feed_give0, grad_attn0, sent, feed_vec0, up0 = call(
        functools.partial(feed_backward, feed_parts0, out_at),
        "feed_backward_0",
        (
            stage_like(len(feeds)),
            stage_like(len(feeds)),
            like(rows, width),
            low_like(slots, width),
            like(4, width),
            like(1, units),
        ),
        (
            place, mixed0, attn0, grad_cpe, own, from_before, from_after, rows_of[0], vec0, up_bias0, *feed_refs0,
        ),
        [*feed_scratch, stage_scratch(len(feeds)), scratch((rows, width), F32)],
    )
    travel = (NEAR, groups // NEAR, chunks + len(feeds), piece, half)
    if direct:
        keep1, give1 = call(
            functools.partial(last_gradients, zbits, in_at),
            "stencil_weights_1",
            (low_like(*travel), low_like(*travel)),
            (
                place, padded1, near_row, grad_first, grad_mixing, rest_keep1, rest_give1,
                feed_keep0, feed_give0,
                mixing_vec1, norm_vec1, feed_vec1, bias1, up1,
            ),
            [
                scratch((kernel * width, rows)),
                stage_scratch(in_at + 1),
                scratch((16, width), F32),
                scratch((piece, half), F32),
            ],
        )
    else:
        front_keep1, front_give1 = call(
            last_weights_back,
            "stencil_weights_1",
            (stage_like(in_at), stage_like(in_at)),
            (place, padded1, near_row, grad_first, grad_mixing),
            [scratch((kernel * width, rows)), stage_scratch(in_at)],
        )
        small_keep, small_give = small_chunk(mixing_vec1, norm_vec1, feed_vec1, bias1, up1)
        there = jnp.array([offset(i, zbits) // NEAR for i in range(groups // NEAR)], jnp.int32) ^ (position // NEAR)

        def in_travel(*values):
            value = jnp.concatenate(values, axis=1).reshape(-1, NEAR, *travel[2:])
            return value[there].swapaxes(0, 1)

        keep1 = in_travel(as_shards(front_keep1), as_shards(rest_keep1, ups), small_keep, as_shards(feed_keep0, ups))
        give1 = in_travel(as_shards(front_give1), as_shards(rest_give1, ups), small_give, as_shards(feed_give0, ups))
    grad_patch_out, sum1 = together(to_all(sent, groups), across(keep1, give1))
    sum1 = lax.psum_scatter(sum1, "near", scatter_dimension=0, tiled=True)
    output = call(
        collect,
        "collect",
        (like(rows, width),),
        (output_back, cols_of[1]),
    )[0]
    grad_in0, bias0, grad_patch = call(
        functools.partial(attention_backward, parts0[1:], in_at),
        "attention_backward_0",
        (low_like(width, 3 * width), like(2, width), low_like(slots, width)),
        (place, patch0, grad_patch_out, rows0, inverse0, powers0, vec0, *refs_b),
        [
            scratch((width, 3 * width)),
            wide_low,
            tall_low,
            tall_low,
            lane_rows,
            wide_low,
            wide_low,
            powers,
            head_rows,
            tall,
            flat,
            flat,
            four_sems,
        ],
        outside=(5,),
    )
    returned, sum1, output = together(to_all(grad_patch, groups), sum1[0], output)
    split = (out_at + 1) // 2
    if direct:
        orders = [(0, split, near_last[0]), (split, out_at + 1 - split, near_last[1])]
        *front0, grad_cpe, grad_first = call(
            functools.partial(first_gradients, parts0, orders, in_at),
            "stencil_weights_0",
            (
                *[stage_like(number) for _, number, _ in orders for _ in range(2)],
                like(rows, width),
                low_like(rows, width),
            ),
            (
                place, returned, cols_of[0], grad_attn0, cpe0, first0, padded0, near_row, vec0, grad_in0,
                feed_vec0, bias0, up0, *refs0,
            ),
            [
                scratch((width, width)),
                scratch((kernel * width, rows)),
                stage_scratch(out_at + 1),
                scratch((4, width), F32),
                scratch((2, width), F32),
                scratch((16, width), F32),
                scratch((piece, half), F32),
            ],
        )
    else:
        keep0, give0, grad_cpe, grad_first, mixing_vec0, norm_vec0 = call(
            functools.partial(first_weights_back, parts0, [(0, out_at, None)]),
            "stencil_weights_0",
            (
                stage_like(out_at),
                stage_like(out_at),
                like(rows, width),
                low_like(rows, width),
                like(4, width),
                like(2, width),
            ),
            (place, returned, cols_of[0], grad_attn0, cpe0, first0, padded0, near_row, vec0, grad_in0, *refs0),
            [scratch((width, width)), scratch((kernel * width, rows)), stage_scratch(out_at)],
        )
        small_keep, small_give = small_chunk(mixing_vec0, norm_vec0, feed_vec0, bias0, up0)
        keep0 = jnp.concatenate([as_shards(keep0), small_keep], axis=1)
        give0 = jnp.concatenate([as_shards(give0), small_give], axis=1)
        front0 = []
        for bits, part in zip(near_last, (slice(0, split), slice(split, out_at + 1))):
            there = jnp.array([offset(i, bits) for i in range(groups)], jnp.int32) ^ position
            front0 += [keep0[there, part], give0[there, part]]
    close = [across(*front0[2 * at : 2 * at + 2]) for at in range(2)]
    grad_first, sum1, *close = together(grad_first, sum1, *close)
    close = [halved(total, bits[-1:]) for total, bits in zip(close, near_last)]
    own, ahead, behind = call(
        functools.partial(first_inputs_back, parts0),
        "stencil_inputs_0",
        (like(rows, width), low_like(HALO, width), low_like(HALO, width)),
        (place, near_row, grad_first, *refs0),
        stencil_back_scratch,
    )
    own, sum1, *close = together(own, halved(sum1, zbits[-1:]), *close)
    close = [halved(total, bits[-2:-1]) for total, bits in zip(close, near_last)]
    sum0 = halved(jnp.concatenate(close, axis=1), zbits[-1:])
    sum0, sum1, ahead, behind = together(sum0, halved(sum1, zbits[:-1]), ahead, behind)
    sum0 = halved(sum0, zbits[:-1])[0]
    sum0 = jnp.concatenate([sum0[:out_at], sum1[0, chunks:], sum0[out_at:]], axis=0)
    sum1 = sum1[0, :chunks]
    grad_inputs = with_rims(grad_cpe, own, *beside(ahead, behind))
    kept_sum = jnp.where(at_first, sum0, sum1)
    other_sum = swap(jnp.where(at_first, sum1, sum0))
    kept = jnp.where(at_first, grad_inputs, output)
    other = swap(jnp.where(at_first, output, grad_inputs))
    boundary_out = jnp.stack([jnp.where(at_first, kept, other), jnp.where(at_first, other, kept)])
    if direct:
        stencil, mixing, grad_in, out, expand, reduce_w, small = call(
            finish,
            "finish",
            (
                like(kernel, piece, width),
                like(piece, width),
                like(piece, 3 * width),
                like(piece, width),
                like(piece, units),
                like(ups * piece, width),
                like(piece, half),
            ),
            (place, kept_sum, other_sum),
        )
        gains, biases, up = small[:3, :piece], small[3:12, :piece], small[12:13, : units // groups]
    else:
        sums = jnp.concatenate(
            [jnp.where(at_first, kept_sum, other_sum), jnp.where(at_first, other_sum, kept_sum)], axis=2
        ).astype(F32)

        def back(chunks):
            return chunks.transpose(1, 0, 2).reshape(piece, -1)

        stencil, mixing, grad_in, out = sums[:kernel], sums[mixing_at], back(sums[in_at:out_at]), sums[out_at]
        expand = back(sums[out_at + 1 : out_at + 1 + ups])
        reduce_w = sums[out_at + 1 + ups : small_at].reshape(ups * piece, width)
        flat = sums[small_at, :, :half].reshape(-1)
        gains, biases = jnp.split(flat[:vectors].reshape(12, piece), [3])
        up = flat[None, vectors : vectors + units // groups]
    grads = (stencil, mixing, grad_in, out, expand, reduce_w, gains, biases)
    return (boundary_out[None], *(grad[None] for grad in grads), up)


def solution(mesh):
    devices = mesh.devices.reshape(mesh.shape["section"], -1, NEAR)
    inner = jax.sharding.Mesh(devices, ("section", *POINTS))
    in_specs = (
        P("section", None, POINTS, None),
        P("section", None, POINTS, None),
        P("section", POINTS, None),
        P("section", POINTS, None),
        P("section", POINTS, None),
        P("section", POINTS, None),
        P("section", POINTS, None),
        P("section", None, POINTS),
        P("section", None, POINTS),
        P("section", POINTS),
        P("section", None, POINTS, None),
        P(None, POINTS, None),
    )
    out_specs = (
        P("section", None, POINTS, None),
        P("section", None, POINTS, None),
        P("section", POINTS, None),
        P("section", POINTS, None),
        P("section", POINTS, None),
        P("section", POINTS, None),
        P("section", POINTS, None),
        P("section", None, POINTS),
        P("section", None, POINTS),
        P("section", POINTS),
    )
    return jax.shard_map(shards, mesh=inner, in_specs=in_specs, out_specs=out_specs, check_vma=False)
```

```python
import functools
import math

import jax
import jax.numpy as jnp
from jax import lax
from jax.experimental import pallas as pl
from jax.experimental.pallas import tpu as pltpu
from jax.sharding import PartitionSpec as P

HEADS = 16
HALO = 64
EPS = 1e-05
NEGATIVE = -1e30
LOWEST = -1e29
LOG2E = 1.4426950408889634
BLOCK = 128
WINDOW = BLOCK + 2 * HALO
LANES = 128
WIDTH = 256
STEP = 256
WIDE_STEP = 384
ABSENT = -(1 << 20)
NEAR = 4
POINTS = ("far", "near")
F32 = jnp.float32
BF16 = jnp.bfloat16


def dot(left, right):
    return jnp.dot(left, right, preferred_element_type=F32)


def dot_tn(left, right):
    return lax.dot_general(left, right, (((0,), (0,)), ((), ())), preferred_element_type=F32)


def dot_nt(left, right):
    return lax.dot_general(left, right, (((1,), (1,)), ((), ())), preferred_element_type=F32)


def dot_tt(left, right):
    return lax.dot_general(left, right, (((0,), (1,)), ((), ())), preferred_element_type=F32)


def iota(shape, dim):
    return lax.broadcasted_iota(jnp.int32, shape, dim)


def norm_parts(rows):
    centred = rows - jnp.mean(rows, axis=-1, keepdims=True)
    spread = jnp.mean(centred * centred, axis=-1, keepdims=True)
    scale = lax.rsqrt(spread + EPS)
    return centred * scale, scale


def norm(rows, gain, shift):
    return norm_parts(rows)[0] * gain + shift


def norm_back(unit, scale, gain, grad):
    inner = grad * gain
    first = jnp.mean(inner, axis=-1, keepdims=True)
    second = jnp.mean(inner * unit, axis=-1, keepdims=True)
    rows = scale * (inner - first - unit * second)
    return rows, column_sum(grad * unit), column_sum(grad)


def column_sum(rows):
    return jnp.sum(rows, axis=0, keepdims=True)


def gelu_parts(inputs):
    cdf = 0.5 + 0.5 * lax.erf(inputs * (0.5**0.5))
    density = jnp.exp(inputs * inputs * -0.5) * (1.0 / math.sqrt(2.0 * math.pi))
    return inputs * cdf, cdf + inputs * density


def gelu(inputs):
    return inputs * (0.5 + 0.5 * lax.erf(inputs * (0.5**0.5)))


GAIN = 0
BIAS = 3


def offset(index, bits):
    return sum(bit for at, bit in enumerate(bits) if index >> at & 1)


def index_of(distance, bits):
    index = 0
    for at, bit in enumerate(bits):
        index = index + ((distance >> (bit.bit_length() - 1)) & 1) * (1 << at)
    return index


def shard_index(shard, position, bits):
    if bits is None:
        return shard
    return index_of(shard ^ position, bits)


class Weights:
    def __init__(self, parts, refs, place):
        self.parts, self.refs = parts, refs
        self.section, self.position = place[0], place[1]

    def find(self, chunk):
        for number, (chunks, bits) in enumerate(self.parts):
            if chunk in chunks:
                return number, chunks.index(chunk), bits
        raise KeyError(chunk)

    def count(self, chunk):
        return self.refs[2 * self.find(chunk)[0]].shape[0]

    def shards(self, chunk):
        number, local, bits = self.find(chunk)
        ref = self.refs[2 * number]
        for shard in range(ref.shape[0]):
            yield shard, ref[shard_index(shard, self.position, bits), local]

    def pieces(self, chunk):
        number, local, bits = self.find(chunk)
        for ref, half in zip(self.refs[2 * number : 2 * number + 2], (self.section, 1 - self.section)):
            for shard in range(ref.shape[0]):
                yield shard, half, ref[shard_index(shard, self.position, bits), local]

    def square(self, target, row, column, chunk):
        for shard, half, value in self.pieces(chunk):
            piece, lanes = value.shape
            at = pl.ds(pl.multiple_of(column + half * lanes, lanes), lanes)
            target[row + shard * piece : row + (shard + 1) * piece, at] = value

    def wide(self, target, chunk):
        rows, width = target.shape
        for at in range(width // rows):
            self.square(target, 0, at * rows, chunk + at)

    def tall(self, target, chunk):
        count = target.shape[0] // target.shape[1]
        for step in range(count):
            for shard, half, value in self.pieces(chunk + step):
                piece, lanes = value.shape
                row = (shard * count + step) * piece
                target[row : row + piece, pl.ds(pl.multiple_of(half * lanes, lanes), lanes)] = value


def pack(stage, chunk, value):
    _, shards, _, piece, lanes = stage.shape
    for half in range(2):
        stage[half, :, chunk] = value[:, half * lanes : (half + 1) * lanes].reshape(shards, piece, lanes)


def pack_rows(stage, chunk, count, value):
    _, shards, _, piece, lanes = stage.shape
    for half in range(2):
        for shard in range(shards):
            for step in range(count):
                row = (shard * count + step) * piece
                stage[half, shard, chunk + step] = value[row : row + piece, half * lanes : (half + 1) * lanes]


def pack_wide(stage, chunk, value):
    rows, width = value.shape
    for at in range(width // rows):
        pack(stage, chunk + at, value[:, at * rows : (at + 1) * rows])


def pack_small(stage, chunk, mixing_vec, norm_vec, feed_vec, bias, up, vec, tile):
    _, shards, _, piece, lanes = stage.shape
    units = up.shape[1] // shards
    sources = (
        (mixing_vec, 0, 0, 1), (norm_vec, 0, 1, 1), (feed_vec, 0, 2, 1), (mixing_vec, 1, 3, 3),
        (norm_vec, 1, 6, 1), (bias, 0, 7, 2), (feed_vec, 1, 9, 3),
    )
    for ref, first, row, count in sources:
        vec[row : row + count, :] = ref[first : first + count, :]
    tile[...] = jnp.zeros(tile.shape, F32)
    for shard in range(shards):
        tile[:12, :piece] = vec[:12, shard * piece : (shard + 1) * piece]
        tile[12:13, :units] = up[:, shard * units : (shard + 1) * units]
        stage[0, shard, chunk] = tile[...].astype(BF16)
        stage[1, shard, chunk] = jnp.zeros((piece, lanes), BF16)


def hand_out(stage, place, outs, orders=None):
    section = place[0]
    if orders is None:
        outs[0][...] = stage[section]
        outs[1][...] = stage[1 - section]
        return
    for number, (first, count, bits) in enumerate(orders):
        for out, half in zip(outs[2 * number : 2 * number + 2], (section, 1 - section)):
            for index in range(out.shape[0]):
                shard = index if bits is None else place[1] ^ offset(index, bits)
                out[index] = stage[half, shard, first : first + count]


def vector(vec_ref, index):
    return vec_ref[index : index + 1, :]


def one_hot(condition):
    return condition.astype(F32).astype(BF16)


def slot_hot(place_row, slots):
    return one_hot(iota((slots, place_row.shape[1]), 0) == place_row[...])


def gather_hot(place_col, slots):
    return one_hot(iota((place_col.shape[0], slots), 1) == place_col[...])


def cut_shards(
    place, stencil, mixing, project_in, project_out, expand, reduce_w, keep_out, give_out
):
    kernel, piece, width = stencil.shape
    half = width // 2
    for out, which in ((keep_out, place[0]), (give_out, 1 - place[0])):
        start = pl.multiple_of(which * half, half)
        out[:kernel] = stencil[:, :, pl.ds(start, half)].astype(BF16)
        at = kernel
        for ref in (mixing, project_in, project_out, expand):
            for step in range(ref.shape[1] // width):
                out[at] = ref[:, pl.ds(pl.multiple_of(step * width + start, half), half)].astype(BF16)
                at += 1
        for step in range(reduce_w.shape[0] // piece):
            out[at] = reduce_w[step * piece : (step + 1) * piece, pl.ds(start, half)].astype(BF16)
            at += 1


def prepare(groups, capacity, target_row, target_col, cotangent, row_out, col_out, count_out, sent_out):
    rows = target_col.shape[0]
    earlier = one_hot(iota((rows, rows), 0) > iota((rows, rows), 1))
    later = one_hot(iota((rows, rows), 0) < iota((rows, rows), 1))
    for block in range(2):
        target = target_col[:, block : block + 1]
        hot = one_hot(iota((rows, groups), 1) == target)
        order = jnp.sum(dot(earlier, hot) * hot.astype(F32), axis=1, keepdims=True)
        col_out[:, block : block + 1] = target * capacity + order.astype(jnp.int32)
        count_out[block : block + 1, :] = column_sum(hot.astype(F32)).astype(jnp.int32)
        target = target_row[block : block + 1, :]
        hot = one_hot(iota((groups, rows), 0) == target)
        order = jnp.sum(dot(hot, later) * hot.astype(F32), axis=0, keepdims=True)
        row_out[block : block + 1, :] = target * capacity + order.astype(jnp.int32)
    hot = one_hot(iota((sent_out.shape[0], rows), 0) == row_out[1:2, :])
    sent_out[...] = dot(hot, cotangent[...]).astype(BF16)


def stencil_forward(parts, small_at, normed_sent, place, before, rows_in, after, near, place_row, *refs):
    if small_at is None:
        vectors_in, refs = refs[:3], refs[3:]
    halves, refs = refs[: 2 * len(parts)], refs[2 * len(parts) :]
    vec, up_bias, columns, padded, *refs = refs
    if normed_sent:
        first_out, cpe_out, sent_out, picked, weight, mixing = refs
    else:
        first_out, sent_out, picked, weight, mixing = refs
    rows, kernel = near.shape
    width = padded.shape[1]
    padded[:HALO, :] = before[...]
    padded[HALO : HALO + rows, :] = rows_in[...]
    padded[HALO + rows :, :] = after[...]
    chunk = 9
    weights = Weights(parts, halves, place)
    if small_at is None:
        vec[...], up_bias[...], columns[...] = (ref[...] for ref in vectors_in)
    else:
        for shard, value in weights.shards(small_at):
            piece, units = width // weights.count(small_at), up_bias.shape[1] // weights.count(small_at)
            value = value.astype(F32)
            vec[:, shard * piece : (shard + 1) * piece] = value[:12, :piece]
            up_bias[:, shard * units : (shard + 1) * units] = value[12:13, :units]
        wide = jnp.concatenate([vec[...], jnp.zeros((LANES - 12, width), F32)], axis=0).T
        columns[...] = wide[:, BIAS + 4 : BIAS + 6]
    for k in range(kernel):
        weights.square(weight, k * width, 0, k)
    weights.square(mixing, 0, 0, kernel)
    for block in range(rows // BLOCK):
        here = slice(block * BLOCK, (block + 1) * BLOCK)
        window = padded[block * BLOCK : block * BLOCK + WINDOW, :]
        lane = iota((BLOCK, WINDOW), 1) + block * BLOCK
        for low in range(0, kernel, chunk):
            ks = range(low, min(low + chunk, kernel))
            hot = jnp.concatenate([one_hot(near[here, k : k + 1] == lane) for k in ks], axis=0)
            got = dot(hot, window).astype(BF16)
            for at, k in enumerate(ks):
                picked[here, k * width : (k + 1) * width] = got[at * BLOCK : (at + 1) * BLOCK, :]
    first_low = (dot(picked[...], weight[...]) + vector(vec, BIAS)).astype(BF16)
    first_out[...] = first_low
    second = dot(first_low, mixing[...]) + vector(vec, BIAS + 1)
    inputs = padded[HALO : HALO + rows, :].astype(F32)
    cpe = inputs + norm(second, vector(vec, GAIN), vector(vec, BIAS + 2))
    if normed_sent:
        cpe_out[...] = cpe
        cpe = norm(cpe, vector(vec, GAIN + 1), vector(vec, BIAS + 3))
    sent_out[...] = dot(slot_hot(place_row, sent_out.shape[0]), cpe.astype(BF16)).astype(BF16)


def high_low(value):
    high = value.astype(BF16)
    return high, (value - high.astype(F32)).astype(BF16)


def of_head(group, head, size):
    return jnp.where(iota(group.shape, 1) // size == head % (LANES // size), group, jnp.zeros((), group.dtype))


def group_lanes(head, size):
    return pl.ds(pl.multiple_of(head * size // LANES * LANES, LANES), LANES)


def spread_heads(target, wide, narrow, ones):
    size = wide[0].shape[1] // HEADS
    sources = (*wide, *narrow)
    row, lane = iota((len(sources) * LANES, LANES), 0), iota((len(sources) * LANES, LANES), 1)
    first = len(wide) * size
    extra = ((iota((1, LANES), 1) >= first + len(narrow)) & (iota((1, LANES), 1) < first + len(narrow) + ones)).astype(F32)
    for head in range(HEADS):
        at, inner = (head * size) // LANES * LANES, (head * size) % LANES
        move = (lane < first) & (row == inner + lane % size + LANES * (lane // size))
        for number in range(len(narrow)):
            move = move | ((lane == first + number) & (row == inner + LANES * (len(wide) + number)))
        both = jnp.concatenate([source[:, at : at + LANES] for source in sources], axis=1)
        target[:, head * LANES : (head + 1) * LANES] = (dot(both, one_hot(move)) + extra).astype(BF16)


def project(patch, weight, vec, query_all, queries, key_all, key_rows, value_rows):
    width = patch.shape[1]
    query = (dot(patch, weight[:, :width]) + vector(vec, BIAS + 4)).astype(BF16)
    if query_all is not None:
        query_all[...] = query.T
    if queries is not None:
        high, low = high_low(query.astype(F32) * ((width // HEADS) ** -0.5 * LOG2E))
        spread_heads(queries, (high, low), (), 1)
    key_rows[...] = dot(patch, weight[:, width : 2 * width]).astype(BF16)
    if key_all is not None:
        key_all[...] = key_rows[...].T
    value_rows[...] = (dot(patch, weight[:, 2 * width :]) + vector(vec, BIAS + 5)).astype(BF16)


def four_powers(source, target, sems, four):
    count = source.shape[0] // (HEADS // 4)
    rows = pl.ds(pl.multiple_of(four * count, count), count)
    return pltpu.make_async_copy(source.at[rows], target.at[rows], sems.at[four])


def attend(queries, key_all, value_rows, mask_row, key, out, inverse_out, powers, powers_out=None, sems=None):
    slots, width = out.shape
    size = width // HEADS
    key[...] = jnp.zeros(key.shape, BF16)
    key[2 * size : 3 * size, :] = jnp.where(iota((size, slots), 0) == 0, mask_row, 0.0).astype(BF16)

    def one_head(shifted, head, carry):
        least, most = carry
        here = pl.ds(pl.multiple_of(head * size, size), size)
        key[:size, :] = key_all[here, :]
        key[size : 2 * size, :] = key_all[here, :]
        lanes, group = pl.ds(pl.multiple_of(head * LANES, LANES), LANES), group_lanes(head, size)
        value = jnp.concatenate([of_head(value_rows[:, group], head, size), jnp.ones((slots, LANES), BF16)], axis=1)
        for start in range(0, slots, WIDE_STEP):
            part = slice(start, start + WIDE_STEP)
            scores = dot(queries[part, lanes], key[...])
            if shifted:
                scores = scores - jnp.max(scores, axis=1, keepdims=True)
            power = jnp.exp2(scores).astype(BF16)
            powers[pl.ds(pl.multiple_of(head * slots + start, WIDE_STEP), WIDE_STEP), :] = power
            both = dot(power, value)
            total = both[:, LANES:]
            least = jnp.minimum(least, jnp.min(total, axis=0, keepdims=True))
            most = jnp.maximum(most, jnp.max(total, axis=0, keepdims=True))
            inverse = 1.0 / total
            out[part, group] += both[:, :LANES] * inverse
            inverse_out[part, group] += of_head(inverse, head, size)
        return least, most

    def four_heads(four, carry):
        carry = functools.reduce(lambda state, at: one_head(False, 4 * four + at, state), range(4), carry)
        if powers_out is not None:
            four_powers(powers, powers_out, sems, four).start()
        return carry

    def clear():
        out[...] = jnp.zeros(out.shape, F32)
        inverse_out[...] = jnp.zeros(inverse_out.shape, F32)

    clear()
    start = (jnp.full((1, LANES), 1.0, F32), jnp.full((1, LANES), 1.0, F32))
    least, most = lax.fori_loop(0, HEADS // 4, four_heads, start)
    if powers_out is not None:
        for four in range(HEADS // 4):
            four_powers(powers, powers_out, sems, four).wait()

    @pl.when(jnp.logical_not((jnp.min(least) > 2.0**-60) & (jnp.max(most) < 2.0**60)))
    def _():
        clear()
        lax.fori_loop(0, HEADS, functools.partial(one_head, True), start)
        if powers_out is not None:
            for four in range(HEADS // 4):
                four_powers(powers, powers_out, sems, four).start()
            for four in range(HEADS // 4):
                four_powers(powers, powers_out, sems, four).wait()


def attend_back(
    grad_rows, out, inverse, query_all, key_rows, value_rows, grads, value_all, grad_all, powers, value,
    grad_query, grad_key, grad_value, powers_in=None, sems=None,
):
    slots, width = out.shape
    size = width // HEADS
    grad_full, scale = grad_rows[...].astype(F32), inverse[...]
    high, low = high_low(grad_full * scale)
    same = one_hot(iota((width, width), 0) // size == iota((width, width), 1) // size)
    inner_high, inner_low = high_low(grad_full * out[...])
    less_high, less_low = high_low(-(dot(inner_high, same) + dot(inner_low, same)) * scale)
    spread_heads(grads, (high, low), (less_high, less_low), 0)
    grad_all[...] = high.T
    value_all[...] = value_rows[...].T
    value[...] = jnp.zeros(value.shape, BF16)
    value[2 * size : 3 * size, :] = one_hot(iota((size, slots), 0) < 2)
    grad_query[...] = jnp.zeros(grad_query.shape, F32)

    def one_head(head):
        here = pl.ds(pl.multiple_of(head * size, size), size)
        value[:size, :] = value_all[here, :]
        value[size : 2 * size, :] = value_all[here, :]
        lanes, group = pl.ds(pl.multiple_of(head * LANES, LANES), LANES), group_lanes(head, size)
        key_head = of_head(key_rows[:, group], head, size)
        query_head, grad_head = query_all[here, :], grad_all[here, :]
        toward_key = jnp.zeros((size, slots), F32)
        toward_value = jnp.zeros((size, slots), F32)
        for start in range(0, slots, STEP):
            part = slice(start, start + STEP)
            power = powers[pl.ds(pl.multiple_of(head * slots + start, STEP), STEP), :]
            change = (power.astype(F32) * dot(grads[part, lanes], value[...])).astype(BF16)
            toward_value += dot(grad_head[:, part], power)
            toward_key += dot(query_head[:, part], change)
            grad_query[part, group] += dot(change, key_head) * size**-0.5
        grad_key[here, :] = toward_key * size**-0.5
        grad_value[here, :] = toward_value

    def four_heads(four, carry):
        if powers_in is not None:
            four_powers(powers_in, powers, sems, four).wait()
        for at in range(4):
            one_head(4 * four + at)
        return carry

    lax.fori_loop(0, HEADS // 4, four_heads, 0)


def attention_forward(parts, chunk, place, patch_in, mask_row, vec, *refs):
    halves, refs = refs[: 2 * len(parts)], refs[2 * len(parts) :]
    low_out, out, inverse_out, powers_out, weight, queries, key_all, key_rows, value_rows, key, powers, sems = refs
    Weights(parts, halves, place).wide(weight, chunk)
    project(patch_in[...], weight, vec, None, queries, key_all, key_rows, value_rows)
    attend(queries, key_all, value_rows, mask_row[...], key, out, inverse_out, powers, powers_out, sems)
    low_out[...] = out[...].astype(BF16)


def attention_outputs(grad_query, grad_key, grad_value, patch, weight, grad_bias_out):
    grad_values = grad_value[...].T
    grad_bias_out[0:1, :] = column_sum(grad_query[...])
    grad_bias_out[1:2, :] = column_sum(grad_values)
    low_grads = jnp.concatenate([grad_query[...], grad_key[...].T, grad_values], axis=1).astype(BF16)
    return dot_tn(patch, low_grads).astype(BF16), dot_nt(low_grads, weight[...]).astype(BF16)


def attention_backward(parts, chunk, place, patch_in, grad_in, out_in, inverse_in, powers_in, vec, *refs):
    halves, refs = refs[: 2 * len(parts)], refs[2 * len(parts) :]
    grad_weight_out, grad_bias_out, grad_patch_out, *refs = refs
    weight, query_all, key_rows, value_rows, grads, value_all, grad_all, powers, value, *refs = refs
    grad_query, grad_key, grad_value, sems = refs
    for four in range(HEADS // 4):
        four_powers(powers_in, powers, sems, four).start()
    patch = patch_in[...]
    Weights(parts, halves, place).wide(weight, chunk)
    project(patch, weight, vec, query_all, None, None, key_rows, value_rows)
    attend_back(
        grad_in, out_in, inverse_in, query_all, key_rows, value_rows, grads, value_all, grad_all, powers, value,
        grad_query, grad_key, grad_value, powers_in, sems,
    )
    grad_weight_out[...], grad_patch_out[...] = attention_outputs(
        grad_query, grad_key, grad_value, patch, weight, grad_bias_out
    )


def unpack_feed(weights, chunk, project, expand, reduce_w):
    weights.wide(project, chunk)
    weights.wide(expand, chunk + 1)
    weights.tall(reduce_w, chunk + 1 + expand.shape[1] // expand.shape[0])


def feed_forward(parts, chunk, place, returned, place_col, cpe, vec, up_bias, *refs):
    halves, refs = refs[: 2 * len(parts)], refs[2 * len(parts) :]
    mixed_out, attn_out, low_out, first_out, last_out, project, expand, reduce_w = refs
    unpack_feed(Weights(parts, halves, place), chunk, project, expand, reduce_w)
    mixed = dot(gather_hot(place_col, returned.shape[0]), returned[...]).astype(BF16)
    mixed_out[...] = mixed
    attn = cpe[...] + dot(mixed, project[...]) + vector(vec, BIAS + 6)
    attn_out[...] = attn
    hidden = norm(attn, vector(vec, GAIN + 2), vector(vec, BIAS + 7)).astype(BF16)
    gated = gelu(dot(hidden, expand[...]) + up_bias[...]).astype(BF16)
    low = (attn + dot(gated, reduce_w[...]) + vector(vec, BIAS + 8)).astype(BF16)
    low_out[...] = low
    first_out[...] = low[:HALO, :]
    last_out[...] = low[-HALO:, :]


def feed_back(mixed, attn, grad_low, project, expand, reduce_w, vec, up_bias, stage, chunk, grad_vec_out, grad_up_out):
    unit, scale = norm_parts(attn)
    hidden = (unit * vector(vec, GAIN + 2) + vector(vec, BIAS + 7)).astype(BF16)
    gated_full, slope = gelu_parts(dot(hidden, expand[...]) + up_bias[...])
    gated = gated_full.astype(BF16)
    grad_full = grad_low.astype(F32)
    grad_up = dot_nt(grad_low, reduce_w[...]) * slope
    grad_up_out[...] = column_sum(grad_up)
    grad_up_low = grad_up.astype(BF16)
    grad_rows, grad_gain, grad_shift = norm_back(
        unit, scale, vector(vec, GAIN + 2), dot_nt(grad_up_low, expand[...])
    )
    grad_attn = grad_full + grad_rows
    grad_attn_low = grad_attn.astype(BF16)
    grad_mixed = dot_nt(grad_attn_low, project[...]).astype(BF16)
    count = expand.shape[1] // expand.shape[0]
    pack_wide(stage, chunk, dot_tn(mixed, grad_attn_low).astype(BF16))
    pack_wide(stage, chunk + 1, dot_tn(hidden, grad_up_low).astype(BF16))
    pack_rows(stage, chunk + 1 + count, count, dot_tn(gated, grad_low).astype(BF16))
    grad_vec_out[0:1, :] = grad_gain
    grad_vec_out[1:2, :] = column_sum(grad_attn)
    grad_vec_out[2:3, :] = grad_shift
    grad_vec_out[3:4, :] = column_sum(grad_full)
    return gated, grad_attn, grad_mixed


def feed_backward(
    parts, chunk, place, mixed, attn, grad_cpe, own, before, after, place_row, vec, up_bias, *refs
):
    halves, refs = refs[: 2 * len(parts)], refs[2 * len(parts) :]
    keep_out, give_out, grad_attn_out, sent_out, grad_vec_out, grad_up_out, project, expand, reduce_w, stage, whole = refs
    whole[...] = own[...]
    whole[:HALO, :] += before[...].astype(F32)
    whole[-HALO:, :] += after[...].astype(F32)
    grad_low = (grad_cpe[...] + whole[...].astype(BF16).astype(F32)).astype(BF16)
    unpack_feed(Weights(parts, halves, place), chunk, project, expand, reduce_w)
    _, grad_attn_out[...], grad_mixed = feed_back(
        mixed[...], attn[...], grad_low, project, expand, reduce_w, vec, up_bias, stage, 0, grad_vec_out, grad_up_out
    )
    sent_out[...] = dot(slot_hot(place_row, sent_out.shape[0]), grad_mixed).astype(BF16)
    hand_out(stage, place, (keep_out, give_out))


def turn_around(parts, chunk, place, patch_in, grad_in, mask, mask_row, vec, up_bias, *refs):
    halves, refs = refs[: 2 * len(parts)], refs[2 * len(parts) :]
    keep_out, give_out, grad_bias_out, grad_patch_out, output_out, grad_vec_out, grad_norm_out, grad_up_out, *refs = refs
    weight, project_out, expand, reduce_w, queries, query_all, key_all, key_rows, value_rows, *refs = refs
    grads, value_all, grad_all, key, out, inverse, powers, grad_query, grad_key, grad_value, stage = refs
    weights = Weights(parts, halves, place)
    weights.wide(weight, chunk)
    unpack_feed(weights, chunk + 3, project_out, expand, reduce_w)
    slots, width = patch_in.shape
    grad_low = grad_in[...]
    rows = patch_in[...].astype(F32)
    unit, scale = norm_parts(rows)
    normed = unit * vector(vec, GAIN + 1) + vector(vec, BIAS + 3)
    patch = jnp.where(mask[...] < 0.0, 0.0, normed).astype(BF16)
    project(patch, weight, vec, query_all, queries, key_all, key_rows, value_rows)
    attend(queries, key_all, value_rows, mask_row[...], key, out, inverse, powers)
    mixed = out[...].astype(BF16)
    attn = rows + dot(mixed, project_out[...]) + vector(vec, BIAS + 6)
    gated, grad_attn, grad_mixed = feed_back(
        mixed, attn, grad_low, project_out, expand, reduce_w, vec, up_bias, stage, 3, grad_vec_out, grad_up_out
    )
    output_out[...] = (attn + dot(gated, reduce_w[...]) + vector(vec, BIAS + 8)).astype(BF16)
    attend_back(
        grad_mixed, out, inverse, query_all, key_rows, value_rows, grads, value_all, grad_all, powers, key,
        grad_query, grad_key, grad_value,
    )
    grad_weight, grad_patch = attention_outputs(grad_query, grad_key, grad_value, patch, weight, grad_bias_out)
    pack_wide(stage, 0, grad_weight)
    hand_out(stage, place, (keep_out, give_out))
    grad_normed = grad_patch.astype(F32)
    unit, scale = norm_parts(rows)
    grad_rows, grad_gain, grad_shift = norm_back(unit, scale, vector(vec, GAIN + 1), grad_normed)
    grad_norm_out[0:1, :] = grad_gain
    grad_norm_out[1:2, :] = grad_shift
    grad_patch_out[...] = (grad_attn + grad_rows).astype(BF16)


def collect(returned, place_col, out):
    out[...] = dot(gather_hot(place_col, returned.shape[0]), returned[...])


def mixing_back(grad_cpe, first, mixing, vec, grad_vec_out):
    first_low = first[...]
    second = dot(first_low, mixing[...]) + vector(vec, BIAS + 1)
    unit, scale = norm_parts(second)
    grad_second, grad_gain, grad_shift = norm_back(unit, scale, vector(vec, GAIN), grad_cpe)
    grad_second_low = grad_second.astype(BF16)
    grad_first = dot_nt(grad_second_low, mixing[...])
    grad_vec_out[0:1, :] = grad_gain
    grad_vec_out[1:2, :] = column_sum(grad_first)
    grad_vec_out[2:3, :] = column_sum(grad_second)
    grad_vec_out[3:4, :] = grad_shift
    return grad_first.astype(BF16), dot_tn(first_low, grad_second_low).astype(BF16)


def stencil_weights_back(padded, near_row, grad_first, stage, picked):
    kernel, rows = near_row.shape
    width = padded.shape[1]
    for block in range(rows // BLOCK):
        here = slice(block * BLOCK, (block + 1) * BLOCK)
        window = padded[block * BLOCK : block * BLOCK + WINDOW, :].T
        row = iota((WINDOW, BLOCK), 0) + block * BLOCK
        for low in range(0, kernel, 2):
            ks = range(low, min(low + 2, kernel))
            hot = jnp.concatenate([one_hot(near_row[k : k + 1, here] == row) for k in ks], axis=1)
            got = dot(window, hot).astype(BF16)
            for at, k in enumerate(ks):
                picked[k * width : (k + 1) * width, here] = got[:, at * BLOCK : (at + 1) * BLOCK]
    step = 3
    for low in range(0, kernel, step):
        got = dot(picked[low * width : (low + step) * width, :], grad_first).astype(BF16)
        for k in range(low, min(low + step, kernel)):
            pack(stage, k, got[(k - low) * width : (k - low + 1) * width, :])


def stencil_inputs_back(near_row, grad_first, weight, own_out, ahead_out, behind_out, toward, total):
    kernel, rows = near_row.shape
    width = weight.shape[1]
    for k in range(kernel):
        toward[k] = dot_nt(grad_first, weight[k * width : (k + 1) * width, :]).astype(BF16)
    total[...] = jnp.zeros(total.shape, F32)
    for block in range(rows // BLOCK):
        here = slice(block * BLOCK, (block + 1) * BLOCK)
        row = iota((WINDOW, BLOCK), 0) + block * BLOCK
        gathered = jnp.zeros((WINDOW, width), F32)
        for low in range(0, kernel, 2):
            ks = range(low, min(low + 2, kernel))
            hot = jnp.concatenate([one_hot(near_row[k : k + 1, here] == row) for k in ks], axis=1)
            gathered += dot(hot, jnp.concatenate([toward[k, here, :] for k in ks], axis=0))
        total[block * BLOCK : block * BLOCK + WINDOW, :] += gathered
    own_out[...] = total[HALO : HALO + rows, :]
    ahead_out[...] = total[:HALO, :].astype(BF16)
    behind_out[...] = total[HALO + rows :, :].astype(BF16)


def unpack_stencil(weights, weight):
    width = weight.shape[1]
    for k in range(weight.shape[0] // width):
        weights.square(weight, k * width, 0, k)


def last_inputs_back(parts, place, returned, place_col, first, near_row, vec, *refs):
    halves, refs = refs[: 2 * len(parts)], refs[2 * len(parts) :]
    grad_cpe_out, own_out, ahead_out, behind_out, grad_first_out, grad_mixing_out, grad_vec_out, *refs = refs
    weight, mixing, toward, total = refs
    weights = Weights(parts, halves, place)
    unpack_stencil(weights, weight)
    weights.square(mixing, 0, 0, near_row.shape[0])
    grad_cpe = dot(gather_hot(place_col, returned.shape[0]), returned[...])
    grad_cpe_out[...] = grad_cpe
    grad_first, grad_mixing_out[...] = mixing_back(grad_cpe, first, mixing, vec, grad_vec_out)
    grad_first_out[...] = grad_first
    stencil_inputs_back(near_row, grad_first, weight, own_out, ahead_out, behind_out, toward, total)


def last_gradients(
    bits, in_at, place, padded, near_row, grad_first, grad_mixing, rest_keep, rest_give, feed_keep, feed_give,
    mixing_vec, norm_vec, feed_vec, bias, up, keep_out, give_out, picked, stage, vec, tile,
):
    stencil_weights_back(padded, near_row, grad_first[...], stage, picked)
    pack(stage, in_at - 1, grad_mixing[...])
    pack_small(stage, in_at, mixing_vec, norm_vec, feed_vec, bias, up, vec, tile)
    section, position = place[0], place[1]
    last = in_at + rest_keep.shape[1]
    for out, half, rest, feed in (
        (keep_out, section, rest_keep, feed_keep),
        (give_out, 1 - section, rest_give, feed_give),
    ):
        for near in range(NEAR):
            for index in range(out.shape[1]):
                shard = ((position // NEAR) ^ (offset(index, bits) // NEAR)) * NEAR + near
                out[near, index, :in_at] = stage[half, shard, :in_at]
                out[near, index, in_at:last] = rest[shard]
                out[near, index, last : last + 1] = stage[half, shard, in_at:]
                out[near, index, last + 1 :] = feed[shard]


def first_gradients(
    parts, orders, in_at, place, returned, place_col, grad_attn, cpe, first, padded, near_row, vec, grad_in,
    feed_vec, bias, up, *refs
):
    halves, refs = refs[: 2 * len(parts)], refs[2 * len(parts) :]
    outs, refs = refs[: 2 * len(orders)], refs[2 * len(orders) :]
    grad_cpe_out, grad_first_out, mixing, picked, stage, mixing_vec, norm_vec, rows, tile = refs
    grad_first, grad_mixing = normed_back(
        parts, halves, place, returned, place_col, grad_attn, cpe, first, near_row.shape[0], vec, mixing,
        grad_cpe_out, grad_first_out, mixing_vec, norm_vec,
    )
    stencil_weights_back(padded, near_row, grad_first, stage, picked)
    pack(stage, in_at - 1, grad_mixing)
    pack_wide(stage, in_at, grad_in[...])
    out_at = in_at + 3
    pack_small(stage, out_at, mixing_vec, norm_vec, feed_vec, bias, up, rows, tile)
    section, position = place[0], place[1]
    for number, (start, count, bits) in enumerate(orders):
        for out, half in zip(outs[2 * number : 2 * number + 2], (section, 1 - section)):
            for index in range(out.shape[0]):
                out[index] = stage[half, position ^ offset(index, bits), start : start + count]


def last_weights_back(place, padded, near_row, grad_first, grad_mixing, keep_out, give_out, picked, stage):
    stencil_weights_back(padded, near_row, grad_first[...], stage, picked)
    pack(stage, near_row.shape[0], grad_mixing[...])
    hand_out(stage, place, (keep_out, give_out))


def normed_back(
    parts, halves, place, returned, place_col, grad_attn, cpe, first, mixing_at, vec, mixing,
    grad_cpe_out, grad_first_out, grad_vec_out, grad_norm_out,
):
    Weights(parts, halves, place).square(mixing, 0, 0, mixing_at)
    grad_normed = dot(gather_hot(place_col, returned.shape[0]), returned[...])
    unit, scale = norm_parts(cpe[...])
    back, grad_gain, grad_shift = norm_back(unit, scale, vector(vec, GAIN + 1), grad_normed)
    grad_norm_out[0:1, :] = grad_gain
    grad_norm_out[1:2, :] = grad_shift
    grad_cpe = grad_attn[...] + back
    grad_cpe_out[...] = grad_cpe
    grad_first, grad_mixing = mixing_back(grad_cpe, first, mixing, vec, grad_vec_out)
    grad_first_out[...] = grad_first
    return grad_first, grad_mixing


def first_weights_back(
    parts, orders, place, returned, place_col, grad_attn, cpe, first, padded, near_row, vec, grad_in, *refs
):
    halves, refs = refs[: 2 * len(parts)], refs[2 * len(parts) :]
    outs, refs = refs[: 2 * len(orders)], refs[2 * len(orders) :]
    grad_cpe_out, grad_first_out, grad_vec_out, grad_norm_out, mixing, picked, stage = refs
    grad_first, grad_mixing = normed_back(
        parts, halves, place, returned, place_col, grad_attn, cpe, first, near_row.shape[0], vec, mixing,
        grad_cpe_out, grad_first_out, grad_vec_out, grad_norm_out,
    )
    stencil_weights_back(padded, near_row, grad_first, stage, picked)
    pack(stage, near_row.shape[0], grad_mixing)
    pack_wide(stage, near_row.shape[0] + 1, grad_in[...])
    hand_out(stage, place, outs, orders)


def finish(place, kept, other, stencil_out, mixing_out, in_out, out_out, expand_out, reduce_out, small_out):
    section = place[0]
    chunks, piece, half = kept.shape
    kernel = stencil_out.shape[0]
    width = 2 * half
    for ref, which in ((kept, section), (other, 1 - section)):
        start = pl.multiple_of(which * half, half)
        stencil_out[:, :, pl.ds(start, half)] = ref[:kernel].astype(F32)
        at = kernel
        for out in (mixing_out, in_out, out_out, expand_out):
            for step in range(out.shape[1] // width):
                out[:, pl.ds(pl.multiple_of(step * width + start, half), half)] = ref[at].astype(F32)
                at += 1
        for step in range(reduce_out.shape[0] // piece):
            reduce_out[step * piece : (step + 1) * piece, pl.ds(start, half)] = ref[at].astype(F32)
            at += 1

    def small(ref):
        small_out[...] = ref[chunks - 1].astype(F32)

    @pl.when(section == 0)
    def _():
        small(kept)

    @pl.when(section == 1)
    def _():
        small(other)


def first_inputs_back(parts, place, near_row, grad_first, *refs):
    halves, refs = refs[: 2 * len(parts)], refs[2 * len(parts) :]
    own_out, ahead_out, behind_out, weight, toward, total = refs
    unpack_stencil(Weights(parts, halves, place), weight)
    stencil_inputs_back(near_row, grad_first[...], weight, own_out, ahead_out, behind_out, toward, total)


class Window:
    def __init__(self, array, first, count):
        self.array, self.first, self.count = array, first, count

    def scratch(self):
        shards, _, piece, lanes = self.array.shape
        return pltpu.VMEM((shards, self.count, piece, lanes), self.array.dtype)


class Outside(jax.ShapeDtypeStruct):
    pass


def call(body, name, outs, args, scratch=(), outside=()):
    windows = [(at, a) for at, a in enumerate(args) if isinstance(a, Window)]
    arrays = [a.array if isinstance(a, Window) else a for a in args]
    spaces = [
        pltpu.SMEM
        if a.shape == (2,)
        else pltpu.HBM
        if isinstance(window, Window)
        else pl.ANY
        if at in outside
        else pltpu.VMEM
        for at, (a, window) in enumerate(zip(arrays, args))
    ]

    def with_windows(*refs):
        refs, copied, sems = list(refs[: -len(windows) - 1]), refs[-len(windows) - 1 : -1], refs[-1]
        copies = []
        for number, (at, window) in enumerate(windows):
            source = refs[at].at[:, window.first : window.first + window.count]
            copies.append(pltpu.make_async_copy(source, copied[number], sems.at[number]))
            copies[-1].start()
            refs[at] = copied[number]
        for copy in copies:
            copy.wait()
        body(*refs)

    extra = [window.scratch() for _, window in windows] + [pltpu.SemaphoreType.DMA((len(windows),))] * bool(windows)
    return pl.pallas_call(
        with_windows if windows else body,
        out_shape=tuple(jax.ShapeDtypeStruct(o.shape, o.dtype) for o in outs),
        in_specs=[pl.BlockSpec(memory_space=space) for space in spaces],
        out_specs=tuple(pl.BlockSpec(memory_space=pl.ANY if isinstance(o, Outside) else pltpu.VMEM) for o in outs),
        scratch_shapes=[*scratch, *extra],
        compiler_params=pltpu.CompilerParams(vmem_limit_bytes=56 * 1024 * 1024),
        cost_estimate=pl.CostEstimate(flops=1, bytes_accessed=1, transcendentals=0),
        name=name,
    )(*arrays)


def like(*shape, dtype=F32):
    return jax.ShapeDtypeStruct(shape, dtype)


def low_like(*shape):
    return jax.ShapeDtypeStruct(shape, BF16)


def swap(value):
    return lax.ppermute(value, "section", [(0, 1), (1, 0)])


def neighbours_along(axis):
    count = lax.axis_size(axis)
    up = [(i, i + 1) for i in range(count - 1)]
    return up, [(j, i) for i, j in up]


def beside(first, last):
    up, down = neighbours_along(POINTS)
    return lax.ppermute(last, POINTS, up), lax.ppermute(first, POINTS, down)


def exchange(pieces):
    return lax.all_to_all(pieces, POINTS, split_axis=0, concat_axis=0, tiled=True)


def to_all(value, groups):
    slots, width = value.shape
    return exchange(value.reshape(groups, slots // groups, width)).reshape(slots, width)


def shards(
    boundary,
    stencil_weight,
    mixing_weight,
    project_in,
    project_out,
    expand_weight,
    reduce_weight,
    norm_gains,
    bias_rows,
    expand_bias,
    patch_index,
    neighbors,
):
    section = lax.axis_index("section")
    groups = lax.axis_size(POINTS)
    position = lax.axis_index(POINTS)
    rows, width = boundary.shape[2:]
    kernel = stencil_weight.shape[1]
    units = expand_weight.shape[2]
    capacity = max(2, 3 * rows // (2 * groups))
    slots = groups * capacity
    size = width // HEADS
    piece = width // groups
    half = width // 2
    ups = units // width
    front_chunks, rest_chunks = kernel + 1, 4 + 2 * ups
    at_first = section == 0
    place = jnp.stack([section, position]).astype(jnp.int32)
    direct = piece % 16 == 0
    chunks = kernel + 6 + 2 * ups
    mixing_at, in_at, out_at, small_at = kernel, kernel + 1, kernel + 4, chunks - 1
    feeds = range(out_at, small_at)
    far = [groups >> at for at in range(1, groups.bit_length())]
    near_last = (far, far[:-2] + far[:-3:-1])

    def of_section(value, which):
        return lax.dynamic_index_in_dim(value, which, 0, keepdims=False)

    def together(*values):
        return lax.optimization_barrier(values)

    def chunks_of(shard):
        return shard.reshape(-1, shard.shape[-1] // width, width).transpose(1, 0, 2).reshape(-1, piece, width)

    if direct:
        own_half, other_half = call(
            cut_shards,
            "cut_shards",
            (low_like(small_at, piece, half), low_like(small_at, piece, half)),
            (
                place,
                stencil_weight[0],
                mixing_weight[0],
                project_in[0],
                project_out[0],
                expand_weight[0],
                reduce_weight[0],
            ),
        )
    else:
        shard = jnp.concatenate(
            [
                stencil_weight[0],
                mixing_weight,
                chunks_of(project_in[0]),
                project_out,
                chunks_of(expand_weight[0]),
                reduce_weight[0].reshape(ups, piece, width),
            ],
            axis=0,
        ).astype(BF16)

        def lanes(value, which):
            return lax.dynamic_slice_in_dim(value, which * half, half, axis=value.ndim - 1)

        own_half, other_half = lanes(shard, section), lanes(shard, 1 - section)
    other_half = swap(other_half)
    halves = (jnp.where(at_first, own_half, other_half), jnp.where(at_first, other_half, own_half))
    halves, boundary, patch_index, neighbors, norm_gains, bias_rows, expand_bias = together(
        halves, boundary, patch_index, neighbors, norm_gains, bias_rows, expand_bias
    )
    if direct:
        small = jnp.concatenate([norm_gains[0], bias_rows[0]], axis=0)
        small = jnp.concatenate(
            [
                jnp.pad(small, ((0, 0), (0, half - piece))),
                jnp.pad(expand_bias, ((0, piece - 13), (0, half - units // groups))),
            ],
            axis=0,
        ).astype(BF16)
    else:
        small = jnp.concatenate([norm_gains[0].reshape(-1), bias_rows[0].reshape(-1), expand_bias[0]])
        small = jnp.pad(small, (0, piece * half - small.shape[0])).reshape(piece, half).astype(BF16)
    other_small = swap(small)
    smalls = (jnp.where(at_first, small, other_small), jnp.where(at_first, other_small, small))

    def partner(value, distance):
        return lax.ppermute(value, POINTS, [(i, i ^ distance) for i in range(groups)])

    def doubled(value, distances):
        for distance in distances:
            value = jnp.concatenate([value, partner(value, distance)], axis=0)
        return value

    def halved(value, distances):
        for distance in distances[::-1]:
            middle = value.shape[0] // 2
            value = (value[:middle].astype(F32) + partner(value[middle:], distance).astype(F32)).astype(BF16)
        return value

    def in_device_order(value, bits):
        return value[shard_index(jnp.arange(groups, dtype=jnp.int32), position, bits)]

    def as_squares(value, numbers):
        tall = len([number for number in numbers if number >= small_at - ups])
        first = len(numbers) - tall
        pieces = [value[:, :first].transpose(1, 0, 2, 3).reshape(first, width, half)]
        if tall:
            pieces.append(value[:, first : first + tall].reshape(tall, width, half))
        return jnp.concatenate(pieces, axis=0)[None]

    def part_of(gathered, numbers, bits):
        numbers = tuple(numbers)
        if not direct:
            numbers = tuple(number for number in numbers if number < small_at)
            gathered = as_squares(gathered if bits is None else in_device_order(gathered, bits), numbers)
            bits = None
        return (gathered, swap(gathered)), (numbers, bits)

    vectors = 12 * piece
    small_part = small_at if direct else None
    vector_likes = (like(12, width), like(1, units), like(width, 2))
    padded_like = low_like(rows + 2 * HALO, width)

    def vectors_of(shards_small):
        if direct:
            return ()
        values = shards_small.reshape(groups, -1)
        vec, up = values[:, :vectors].astype(F32).reshape(groups, 12, piece), values[:, vectors : vectors + units // groups]
        vec = vec.transpose(1, 0, 2).reshape(12, width)
        return vec, up.astype(F32).reshape(1, units), jnp.stack([vec[BIAS + 4], vec[BIAS + 5]], axis=1)

    stage_shape = (groups, piece) if direct else (1, width)

    def stage_like(number):
        return low_like(stage_shape[0], number, stage_shape[1], half)

    def stage_scratch(number):
        return pltpu.VMEM((2, stage_shape[0], number, stage_shape[1], half), BF16)

    def as_shards(value, tall=0):
        if direct:
            return value
        first = value.shape[1] - tall
        main = value[0, :first].reshape(first, groups, piece, half).transpose(1, 0, 2, 3)
        return jnp.concatenate([main, value[0, first:].reshape(groups, tall, piece, half)], axis=1)

    def small_chunk(mixing_vec, norm_vec, feed_vec, bias, up):
        vec = jnp.concatenate(
            [mixing_vec[0:1], norm_vec[0:1], feed_vec[0:1], mixing_vec[1:4], norm_vec[1:2], bias, feed_vec[1:4]],
            axis=0,
        )
        vec = vec.reshape(12, groups, piece).transpose(1, 0, 2).reshape(groups, vectors)
        vec = jnp.concatenate([vec, up.reshape(groups, units // groups)], axis=1)
        vec = jnp.pad(vec, ((0, 0), (0, piece * half - vec.shape[1]))).reshape(groups, 1, piece, half).astype(BF16)
        none = jnp.zeros_like(vec)
        return jnp.where(at_first, vec, none), jnp.where(at_first, none, vec)

    def across(keep, give):
        return (keep.astype(F32) + swap(give).astype(F32)).astype(BF16)

    mine = of_section(boundary[0], section)
    theirs = swap(of_section(boundary[0], 1 - section))
    inputs = jnp.where(at_first, mine, theirs)
    cotangent = jnp.where(at_first, theirs, mine)
    index = patch_index[0, :, :, 0]
    own_index = of_section(index, section)
    other_index = swap(of_section(index, 1 - section))
    targets = jnp.stack([jnp.where(at_first, own_index, other_index), jnp.where(at_first, other_index, own_index)])
    linked = of_section(neighbors, section)
    near = jnp.where(linked >= 0, linked - position * rows + HALO, ABSENT)
    near_row = near.T
    place_rows, place_cols, counts, cotangent_sent = call(
        functools.partial(prepare, groups, capacity),
        "prepare",
        (
            like(2, rows, dtype=jnp.int32),
            like(rows, 2, dtype=jnp.int32),
            like(2, groups, dtype=jnp.int32),
            low_like(slots, width),
        ),
        (targets, targets.T, cotangent),
    )
    numbers = jnp.pad(counts.reshape(1, 2 * groups).astype(BF16), ((0, piece - 1), (0, half - 2 * groups)))
    windows = ((0, kernel, 1), (out_at, small_at, 0), (in_at, small_at, 1), (mixing_at, in_at, 1))
    spread = jnp.concatenate([halves[block][first:last] for first, last, block in windows], axis=0)
    spread = lax.all_gather(spread, POINTS, axis=0, tiled=False)

    picked = [*range(out_at), small_at, chunks, chunks + 1]
    middle = len(picked) // 2
    close = doubled(halves[0][None, :out_at], far[:-3])
    late = doubled(jnp.stack([*smalls, numbers])[None], far[:-3])
    close = doubled(jnp.concatenate([close, late], axis=1), far[-3:-2])
    close, near, near_row, inputs = together(close, near, near_row, inputs)
    halo0 = beside(inputs[:HALO], inputs[-HALO:])
    ends = [close[:, :middle], close[:, middle:]]
    rows_of = (place_rows[0:1], place_rows[1:2])
    cols_of = (place_cols[:, 0:1], place_cols[:, 1:2])
    ends = [doubled(end, distances[-2:]) for end, distances in zip(ends, near_last)]
    *halo0, end_a, end_b = together(*halo0, *ends)
    ends = [end_a, end_b]
    zbits = far[:-2]
    refs_a, part_a = part_of(ends[0], picked[:middle], near_last[0])
    refs_b, part_b = part_of(ends[1], picked[middle:], near_last[1])
    refs0, parts0 = (*refs_a, *refs_b), (part_a, part_b)
    vectors0 = vectors_of(in_device_order(ends[1][:, -3], near_last[1]))
    arrived = in_device_order(ends[1][:, -1, 0, : 2 * groups], near_last[1]).reshape(groups, 2, groups)
    arrived = lax.dynamic_index_in_dim(arrived, position, 2, keepdims=False).astype(jnp.int32)
    slot = jnp.arange(slots, dtype=jnp.int32)
    present = (slot % capacity)[:, None] < jnp.repeat(arrived, capacity, axis=0)
    masks = jnp.where(present, 0.0, NEGATIVE).astype(F32)
    mask_rows, masks = masks.T, (masks[:, 0:1], masks[:, 1:2])
    mask_rows = (mask_rows[0:1], mask_rows[1:2])


    def scratch(shape, dtype=BF16):
        return pltpu.VMEM(shape, dtype)

    stencil_scratch = [scratch((rows, kernel * width)), scratch((kernel * width, width)), scratch((width, width))]
    feed_scratch = [scratch((width, width)), scratch((width, units)), scratch((units, width))]
    lane_rows = scratch((slots, HEADS * LANES))
    tall_low = scratch((slots, width))
    tall, flat = scratch((slots, width), F32), scratch((width, slots), F32)
    wide_low = scratch((width, slots))
    head_rows = scratch((LANES, slots))

    vec0, up_bias0, columns0, padded0, first0, cpe0, sent = call(
        functools.partial(stencil_forward, parts0, small_part, True),
        "stencil_forward_0",
        (*vector_likes, padded_like, low_like(rows, width), like(rows, width), low_like(slots, width)),
        (place, halo0[0], inputs, halo0[1], near, rows_of[0], *vectors0, *refs0),
        stencil_scratch,
    )
    patch0 = to_all(sent, groups)
    patch0, cotangent_sent, spread, mask_rows, masks = together(patch0, cotangent_sent, spread, mask_rows, masks)
    cotangent_patch, other_spread = to_all(cotangent_sent, groups), swap(spread)
    powers_like = Outside((HEADS * slots, slots), BF16)
    powers = scratch(powers_like.shape)
    four_sems = pltpu.SemaphoreType.DMA((HEADS // 4,))
    out, rows0, inverse0, powers0 = call(
        functools.partial(attention_forward, parts0[1:], in_at),
        "attention_forward_0",
        (low_like(slots, width), like(slots, width), like(slots, width), powers_like),
        (place, patch0, mask_rows[0], vec0, *refs_b),
        [
            scratch((width, 3 * width)),
            lane_rows,
            wide_low,
            tall_low,
            tall_low,
            head_rows,
            powers,
            four_sems,
        ],
    )
    out, cotangent_patch, other_spread = together(out, cotangent_patch, other_spread)
    returned = to_all(out, groups)
    spread_parts, first = [], 0
    for low, high, block in windows:
        number = high - low
        if direct:
            refs = (Window(spread, first, number), Window(other_spread, first, number))
            spread_parts.append((refs, (tuple(range(low, high)), None)))
        else:
            spread_parts.append(part_of(spread[:, first : first + number], range(low, high), None))
        first += number
    (refs_s, part_s), (feed_refs0, feed_part0), (rest_refs1, rest_part1), (refs_m, part_m) = spread_parts
    refs1, parts1, feed_parts0, rest_parts1 = (*refs_s, *refs_m), (part_s, part_m), (feed_part0,), (rest_part1,)
    forward_refs1, forward_parts1 = refs1, parts1
    if direct:
        at = len(part_b[0]) - 2
        forward_refs1 = (*refs1, *(Window(ref, at, 1) for ref in refs_b))
        forward_parts1 = (*parts1, ((small_at,), near_last[1]))
    vectors1 = vectors_of(in_device_order(ends[1][:, -2], near_last[1]))
    mixed0, attn0, middle, middle_first, middle_last = call(
        functools.partial(feed_forward, feed_parts0, out_at),
        "feed_forward_0",
        (
            low_like(rows, width),
            like(rows, width),
            low_like(rows, width),
            low_like(HALO, width),
            low_like(HALO, width),
        ),
        (place, returned, cols_of[0], cpe0, vec0, up_bias0, *feed_refs0),
        feed_scratch,
    )

    before, after = beside(middle_first, middle_last)
    vec1, up_bias1, columns1, padded1, first1, sent = call(
        functools.partial(stencil_forward, forward_parts1, small_part, False),
        "stencil_forward_1",
        (*vector_likes, padded_like, low_like(rows, width), low_like(slots, width)),
        (place, before, middle, after, near, rows_of[1], *vectors1, *forward_refs1),
        stencil_scratch,
    )
    patch1 = to_all(sent, groups)
    rest_keep1, rest_give1, bias1, grad_patch, output_sent, feed_vec1, norm_vec1, up1 = call(
        functools.partial(turn_around, rest_parts1, in_at),
        "turn_around_1",
        (
            stage_like(3 + len(feeds)),
            stage_like(3 + len(feeds)),
            like(2, width),
            low_like(slots, width),
            low_like(slots, width),
            like(4, width),
            like(2, width),
            like(1, units),
        ),
        (place, patch1, cotangent_patch, masks[1], mask_rows[1], vec1, up_bias1, *rest_refs1),
        [
            scratch((width, 3 * width)),
            *feed_scratch,
            lane_rows,
            wide_low,
            wide_low,
            tall_low,
            tall_low,
            lane_rows,
            wide_low,
            wide_low,
            head_rows,
            tall,
            tall,
            powers,
            tall,
            flat,
            flat,
            stage_scratch(3 + len(feeds)),
        ],
    )
    returned = to_all(grad_patch, groups)

    returned, output_sent = together(returned, output_sent)
    output_back = to_all(output_sent, groups)
    stencil_back_scratch = [
        scratch((kernel * width, width)),
        scratch((kernel, rows, width)),
        scratch((rows + 2 * HALO, width), F32),
    ]
    grad_cpe, own, ahead, behind, grad_first, grad_mixing, mixing_vec1 = call(
        functools.partial(last_inputs_back, parts1),
        "stencil_inputs_1",
        (
            like(rows, width),
            like(rows, width),
            low_like(HALO, width),
            low_like(HALO, width),
            low_like(rows, width),
            low_like(width, width),
            like(4, width),
        ),
        (place, returned, cols_of[1], first1, near_row, vec1, *refs1),
        [stencil_back_scratch[0], scratch((width, width)), *stencil_back_scratch[1:]],
    )

    def with_rims(grad_cpe, own, from_before, from_after):
        empty = jnp.zeros((rows - 2 * HALO, width), F32)
        own = own + jnp.concatenate([from_before.astype(F32), empty, from_after.astype(F32)], axis=0)
        return grad_cpe + own.astype(BF16).astype(F32)

    ahead, output_back = together(ahead, output_back)
    from_before, from_after = beside(ahead, behind)

    feed_keep0, feed_give0, grad_attn0, sent, feed_vec0, up0 = call(
        functools.partial(feed_backward, feed_parts0, out_at),
        "feed_backward_0",
        (
            stage_like(len(feeds)),
            stage_like(len(feeds)),
            like(rows, width),
            low_like(slots, width),
            like(4, width),
            like(1, units),
        ),
        (
            place, mixed0, attn0, grad_cpe, own, from_before, from_after, rows_of[0], vec0, up_bias0, *feed_refs0,
        ),
        [*feed_scratch, stage_scratch(len(feeds)), scratch((rows, width), F32)],
    )
    travel = (NEAR, groups // NEAR, chunks + len(feeds), piece, half)
    if direct:
        keep1, give1 = call(
            functools.partial(last_gradients, zbits, in_at),
            "stencil_weights_1",
            (low_like(*travel), low_like(*travel)),
            (
                place, padded1, near_row, grad_first, grad_mixing, rest_keep1, rest_give1,
                feed_keep0, feed_give0,
                mixing_vec1, norm_vec1, feed_vec1, bias1, up1,
            ),
            [
                scratch((kernel * width, rows)),
                stage_scratch(in_at + 1),
                scratch((16, width), F32),
                scratch((piece, half), F32),
            ],
        )
    else:
        front_keep1, front_give1 = call(
            last_weights_back,
            "stencil_weights_1",
            (stage_like(in_at), stage_like(in_at)),
            (place, padded1, near_row, grad_first, grad_mixing),
            [scratch((kernel * width, rows)), stage_scratch(in_at)],
        )
        small_keep, small_give = small_chunk(mixing_vec1, norm_vec1, feed_vec1, bias1, up1)
        there = jnp.array([offset(i, zbits) // NEAR for i in range(groups // NEAR)], jnp.int32) ^ (position // NEAR)

        def in_travel(*values):
            value = jnp.concatenate(values, axis=1).reshape(-1, NEAR, *travel[2:])
            return value[there].swapaxes(0, 1)

        keep1 = in_travel(as_shards(front_keep1), as_shards(rest_keep1, ups), small_keep, as_shards(feed_keep0, ups))
        give1 = in_travel(as_shards(front_give1), as_shards(rest_give1, ups), small_give, as_shards(feed_give0, ups))
    grad_patch_out, sum1 = together(to_all(sent, groups), across(keep1, give1))
    sum1 = lax.psum_scatter(sum1, "near", scatter_dimension=0, tiled=True)
    output = call(
        collect,
        "collect",
        (like(rows, width),),
        (output_back, cols_of[1]),
    )[0]
    grad_in0, bias0, grad_patch = call(
        functools.partial(attention_backward, parts0[1:], in_at),
        "attention_backward_0",
        (low_like(width, 3 * width), like(2, width), low_like(slots, width)),
        (place, patch0, grad_patch_out, rows0, inverse0, powers0, vec0, *refs_b),
        [
            scratch((width, 3 * width)),
            wide_low,
            tall_low,
            tall_low,
            lane_rows,
            wide_low,
            wide_low,
            powers,
            head_rows,
            tall,
            flat,
            flat,
            four_sems,
        ],
        outside=(5,),
    )
    returned, sum1, output = together(to_all(grad_patch, groups), sum1[0], output)
    split = (out_at + 1) // 2
    if direct:
        orders = [(0, split, near_last[0]), (split, out_at + 1 - split, near_last[1])]
        *front0, grad_cpe, grad_first = call(
            functools.partial(first_gradients, parts0, orders, in_at),
            "stencil_weights_0",
            (
                *[stage_like(number) for _, number, _ in orders for _ in range(2)],
                like(rows, width),
                low_like(rows, width),
            ),
            (
                place, returned, cols_of[0], grad_attn0, cpe0, first0, padded0, near_row, vec0, grad_in0,
                feed_vec0, bias0, up0, *refs0,
            ),
            [
                scratch((width, width)),
                scratch((kernel * width, rows)),
                stage_scratch(out_at + 1),
                scratch((4, width), F32),
                scratch((2, width), F32),
                scratch((16, width), F32),
                scratch((piece, half), F32),
            ],
        )
    else:
        keep0, give0, grad_cpe, grad_first, mixing_vec0, norm_vec0 = call(
            functools.partial(first_weights_back, parts0, [(0, out_at, None)]),
            "stencil_weights_0",
            (
                stage_like(out_at),
                stage_like(out_at),
                like(rows, width),
                low_like(rows, width),
                like(4, width),
                like(2, width),
            ),
            (place, returned, cols_of[0], grad_attn0, cpe0, first0, padded0, near_row, vec0, grad_in0, *refs0),
            [scratch((width, width)), scratch((kernel * width, rows)), stage_scratch(out_at)],
        )
        small_keep, small_give = small_chunk(mixing_vec0, norm_vec0, feed_vec0, bias0, up0)
        keep0 = jnp.concatenate([as_shards(keep0), small_keep], axis=1)
        give0 = jnp.concatenate([as_shards(give0), small_give], axis=1)
        front0 = []
        for bits, part in zip(near_last, (slice(0, split), slice(split, out_at + 1))):
            there = jnp.array([offset(i, bits) for i in range(groups)], jnp.int32) ^ position
            front0 += [keep0[there, part], give0[there, part]]
    close = [across(*front0[2 * at : 2 * at + 2]) for at in range(2)]
    grad_first, sum1, *close = together(grad_first, sum1, *close)
    close = [halved(total, bits[-1:]) for total, bits in zip(close, near_last)]
    own, ahead, behind = call(
        functools.partial(first_inputs_back, parts0),
        "stencil_inputs_0",
        (like(rows, width), low_like(HALO, width), low_like(HALO, width)),
        (place, near_row, grad_first, *refs0),
        stencil_back_scratch,
    )
    own, sum1, *close = together(own, halved(sum1, zbits[-1:]), *close)
    close = [halved(total, bits[-2:-1]) for total, bits in zip(close, near_last)]
    sum0, ahead, behind = together(jnp.concatenate(close, axis=1), ahead, behind)
    sum0, sum1 = together(halved(sum0, zbits[-1:]), halved(sum1, zbits[:-1]))
    sum0 = halved(sum0, zbits[:-1])[0]
    sum0 = jnp.concatenate([sum0[:out_at], sum1[0, chunks:], sum0[out_at:]], axis=0)
    sum1 = sum1[0, :chunks]
    grad_inputs = with_rims(grad_cpe, own, *beside(ahead, behind))
    kept_sum = jnp.where(at_first, sum0, sum1)
    other_sum = swap(jnp.where(at_first, sum1, sum0))
    kept = jnp.where(at_first, grad_inputs, output)
    other = swap(jnp.where(at_first, output, grad_inputs))
    boundary_out = jnp.stack([jnp.where(at_first, kept, other), jnp.where(at_first, other, kept)])
    if direct:
        stencil, mixing, grad_in, out, expand, reduce_w, small = call(
            finish,
            "finish",
            (
                like(kernel, piece, width),
                like(piece, width),
                like(piece, 3 * width),
                like(piece, width),
                like(piece, units),
                like(ups * piece, width),
                like(piece, half),
            ),
            (place, kept_sum, other_sum),
        )
        gains, biases, up = small[:3, :piece], small[3:12, :piece], small[12:13, : units // groups]
    else:
        sums = jnp.concatenate(
            [jnp.where(at_first, kept_sum, other_sum), jnp.where(at_first, other_sum, kept_sum)], axis=2
        ).astype(F32)

        def back(chunks):
            return chunks.transpose(1, 0, 2).reshape(piece, -1)

        stencil, mixing, grad_in, out = sums[:kernel], sums[mixing_at], back(sums[in_at:out_at]), sums[out_at]
        expand = back(sums[out_at + 1 : out_at + 1 + ups])
        reduce_w = sums[out_at + 1 + ups : small_at].reshape(ups * piece, width)
        flat = sums[small_at, :, :half].reshape(-1)
        gains, biases = jnp.split(flat[:vectors].reshape(12, piece), [3])
        up = flat[None, vectors : vectors + units // groups]
    grads = (stencil, mixing, grad_in, out, expand, reduce_w, gains, biases)
    return (boundary_out[None], *(grad[None] for grad in grads), up)


def solution(mesh):
    devices = mesh.devices.reshape(mesh.shape["section"], -1, NEAR)
    inner = jax.sharding.Mesh(devices, ("section", *POINTS))
    in_specs = (
        P("section", None, POINTS, None),
        P("section", None, POINTS, None),
        P("section", POINTS, None),
        P("section", POINTS, None),
        P("section", POINTS, None),
        P("section", POINTS, None),
        P("section", POINTS, None),
        P("section", None, POINTS),
        P("section", None, POINTS),
        P("section", POINTS),
        P("section", None, POINTS, None),
        P(None, POINTS, None),
    )
    out_specs = (
        P("section", None, POINTS, None),
        P("section", None, POINTS, None),
        P("section", POINTS, None),
        P("section", POINTS, None),
        P("section", POINTS, None),
        P("section", POINTS, None),
        P("section", POINTS, None),
        P("section", None, POINTS),
        P("section", None, POINTS),
        P("section", POINTS),
    )
    return jax.shard_map(shards, mesh=inner, in_specs=in_specs, out_specs=out_specs, check_vma=False)
```
